256 devices in a mesh: dp: 32 (over z_lo, y, core), mp: 8 (over x, z_hi).
Axes of the slice: x: 4, y: 4, z: 8 (z_hi: 2, z_lo: 4; z = z_hi * 4 + z_lo), core: 2. Of those that a mesh axis runs over, the one named last changes fastest.
Arguments:
- preactivation: bfloat16 [4096, 14336], P('dp', 'mp'), may hold values from -6 to 6
- keep_codes: int32 [4096, 3584], P('dp', 'mp'), may hold values from 0 to 5
- down_weight: bfloat16 [14336, 4096], P('mp', 'dp'), may hold values from -0.046875 to 0.046875
- output_grad: bfloat16 [4096, 4096], P(('dp', 'mp')), may hold values from -24 to 24
Outputs:
- output: bfloat16 [4096, 4096], P(('dp', 'mp'))
- weight_grad: bfloat16 [14336, 4096], P('mp', 'dp')
- input_grad: bfloat16 [4096, 14336], P('dp', 'mp')
The draws below stay inside these ranges and needn't reach their ends.
Inputs may be any that keep to these rules, and one draw needn't show every extreme that they name: `keep_codes`: code of one token's group of four hidden units.
All inputs are finite; a program needn't handle non-finite values.
Results may differ from the reference program's by a relative error of at most 0.015.
Values may be sent and summed in bfloat16 or wider, within the bound.
No kernel may reach another device: no remote copies, remote signals or barrier semaphores. Data moves between devices by JAX's collectives and lax.ppermute only.
A program may use at most 128 MiB of HBM per device.

```python
import math
import jax
import jax.numpy as jnp
from jax import lax

D = 4096
FF = 14336
TOKENS = 4096
N_MP = 8


def plant(values, own_key, smallest, largest):
    spot = [jax.random.randint(jax.random.fold_in(own_key, axis), (), 0, length) for axis, length in enumerate(values.shape)]
    longest = values.shape.index(max(values.shape))
    neighbour = spot[:longest] + [(spot[longest] + 1) % values.shape[longest]] + spot[longest + 1:]
    return values.at[tuple(spot)].set(smallest).at[tuple(neighbour)].set(largest)


def spiked(entries, own_key, source, target, shards_of, factor):
    owner, partner = [(jnp.arange(entries.shape[axis_at]) // (entries.shape[axis_at] // shards_of)).reshape([-1 if axis == axis_at else 1 for axis in range(entries.ndim)]) for axis_at in (source, target)]
    chosen = jax.random.permutation(own_key, shards_of)[partner]
    strong = (owner == chosen) | (owner == (partner + shards_of // 2) % shards_of)
    return jnp.where(strong, factor * entries, entries)


def steps_of(key, shape, shards, low, largest):
    def one(axis_at, blocks):
        heights = jax.random.uniform(jax.random.fold_in(jax.random.fold_in(key, 6), axis_at), (blocks,), jnp.float32, low / len(shards), largest / len(shards))
        return jnp.repeat(jnp.exp(heights), shape[axis_at] // blocks).reshape((-1,) + (1,) * (len(shape) - axis_at - 1))

    level = one(*shards[0])
    for cut in shards[1:]:
        level = level * one(*cut)
    return level


def normal_values(key, extent, scale, bound, cuts=(), kind=jnp.bfloat16):
    array = scale * jax.random.normal(key, extent, jnp.float32)
    if cuts:
        array = array * steps_of(key, extent, cuts, -0.22, 0.18)
    return jnp.clip(array, -bound, bound).astype(kind)


def gaussian_with(key, shape, scale, bound, split, heavy, dtype=jnp.bfloat16):
    drawn = scale * jax.random.normal(key, shape, jnp.float32)
    if split:
        drawn = drawn * steps_of(key, shape, split, -0.22, 0.18)
    return jnp.clip(spiked(drawn, jax.random.fold_in(key, 3), *heavy), -bound, bound).astype(dtype)


def setup_inputs(seed: int = 0) -> dict:
    splits = jax.random.split(jax.random.key(seed), 5)
    return {
        "preactivation": normal_values(splits[0], (TOKENS, FF), 1.0, 6.0, ((0, 32), (1, 8))),
        "keep_codes": plant(jax.random.randint(splits[1], (TOKENS, FF // 4), 0, 6), jax.random.fold_in(splits[1], 1), 0, 5).astype(jnp.int32),
        "down_weight": normal_values(splits[2], (FF, D), FF ** -0.5, 0.046875, ((0, 8), (1, 32))),
        "output_grad": gaussian_with(splits[3], (TOKENS, D), 1.0, 24.0, ((0, 256),), (0, 1, 256, 6.0)),
    }


PAIRS = ((0, 1), (0, 2), (0, 3), (1, 2), (1, 3), (2, 3))

def keep_mask(codes, width):
    expanded = jnp.repeat(codes, 4, axis=1)
    lane = jnp.arange(width) % 4
    keep = jnp.zeros(expanded.shape, jnp.float32)
    for pattern, pair in enumerate(PAIRS):
        inside = (lane == pair[0]) | (lane == pair[1])
        keep = keep + ((expanded == pattern) & inside[None, :]).astype(jnp.float32)
    return keep

def reference(preactivation, keep_codes, down_weight, output_grad):
    block_width = FF // N_MP
    grad_scale = 1.0 / math.sqrt(TOKENS)
    pre_blocks = preactivation.reshape(TOKENS, N_MP, block_width).transpose(1, 0, 2)
    code_blocks = keep_codes.reshape(TOKENS, N_MP, block_width // 4).transpose(1, 0, 2)
    weight_blocks = down_weight.reshape(N_MP, block_width, D)

    def one_block(inputs):
        pre_block, code_block, weight_block = inputs
        keep = keep_mask(code_block, block_width)
        positive = jnp.maximum(pre_block.astype(jnp.float32), 0.0)
        hidden = (keep * positive * positive).astype(jnp.bfloat16)
        part = jnp.dot(hidden, weight_block, preferred_element_type=jnp.float32).astype(jnp.bfloat16)
        back = jnp.dot(output_grad, weight_block.T, preferred_element_type=jnp.float32)
        pre_grad = (2.0 * positive * keep * back).astype(jnp.bfloat16)
        grad = jnp.dot(hidden.T, output_grad, preferred_element_type=jnp.float32) * grad_scale
        return (part, pre_grad, grad.astype(jnp.bfloat16))
    parts, pre_grads, grads = lax.map(one_block, (pre_blocks, code_blocks, weight_blocks))
    output = lax.optimization_barrier(jnp.sum(parts.astype(jnp.float32), axis=0)).astype(jnp.bfloat16)
    input_grad = pre_grads.transpose(1, 0, 2).reshape(TOKENS, FF)
    weight_grad = grads.reshape(FF, D)
    return (output, weight_grad, input_grad)
```

```python
import math

import jax
import jax.numpy as jnp
from jax import lax
from jax.experimental import pallas as pl
from jax.experimental.pallas import tpu as pltpu
from jax.sharding import PartitionSpec as P

BF16 = jnp.bfloat16
F32 = jnp.float32

CORE = 1
ROWS_Y, ROWS_Z = 2, 16
COLS_Y, COLS_Z = 6, 8
TOKEN_PARTS = (0, ROWS_Y, ROWS_Z, ROWS_Y ^ ROWS_Z)
COLUMN_PARTS = (0, COLS_Y, COLS_Z, COLS_Y ^ COLS_Z)
COLUMN_BLOCKS = COLUMN_PARTS + tuple(k ^ CORE for k in COLUMN_PARTS)
STEP = 256


def swap(array, axis, size, k):
    return lax.ppermute(array, axis, [(i, i ^ k) for i in range(size)])


def dp_swap(array, k):
    return swap(array, "dp", 32, k)


def mp_swap(array, k):
    return swap(array, "mp", 8, k)


def place(axis):
    return jnp.reshape(lax.axis_index(axis).astype(jnp.int32), (1,))


def in_smem():
    return pl.BlockSpec(memory_space=pltpu.SMEM)


def whole():
    return pl.BlockSpec(memory_space=pltpu.VMEM)


def call(kernel, out_shape, scratch=(), grid=None, in_specs=None, out_specs=None, flops=0, moved=0):
    return pl.pallas_call(
        kernel,
        out_shape=out_shape,
        grid=grid or (),
        in_specs=in_specs,
        out_specs=out_specs,
        scratch_shapes=list(scratch),
        compiler_params=pltpu.CompilerParams(vmem_limit_bytes=40 * 2**20),
        cost_estimate=pl.CostEstimate(flops=flops, bytes_accessed=moved, transcendentals=0),
    )


def mask_kernel(pre_ref, code_ref, hidden_ref, slope_ref):
    rows, width = pre_ref.shape
    groups = code_ref.shape[1]
    for at in range(0, groups, 128):
        size = min(128, groups - at)
        spread = (
            lax.broadcasted_iota(jnp.int32, (size, 4 * size), 1) // 4
            == lax.broadcasted_iota(jnp.int32, (size, 4 * size), 0)
        ).astype(BF16)
        codes = code_ref[:, at : at + size].astype(F32).astype(BF16)
        code = jnp.dot(codes, spread, preferred_element_type=F32)
        lane = lax.broadcasted_iota(jnp.int32, code.shape, 1) % 4
        kept = (
            ((lane == 0) & (code < 2.5))
            | ((lane == 1) & ((code == 0.0) | (code == 3.0) | (code == 4.0)))
            | ((lane == 2) & ((code == 1.0) | (code == 3.0) | (code == 5.0)))
            | ((lane == 3) & ((code == 2.0) | (code > 3.5)))
        )
        columns = slice(4 * at, 4 * (at + size))
        positive = jnp.where(kept, jnp.maximum(pre_ref[:, columns].astype(F32), 0.0), 0.0)
        hidden_ref[:, columns] = (positive * positive).astype(BF16)
        slope_ref[:, columns] = (2.0 * positive).astype(BF16)


def split_kernel(place_ref, grad_ref, *out_refs):
    me = place_ref[0]
    for out_ref, token in zip(out_refs, TOKEN_PARTS):
        for n, column in enumerate(COLUMN_BLOCKS):
            at = pl.multiple_of((me ^ (token ^ column)) * 128, 128)
            out_ref[:, n * 128 : (n + 1) * 128] = grad_ref[:, pl.ds(at, 128)]


def join_kernel(place_ref, *refs):
    me = place_ref[0]
    out_ref = refs[-1]
    for part_ref, token in zip(refs[:-1], TOKEN_PARTS):
        for n, column in enumerate(COLUMN_BLOCKS):
            at = pl.multiple_of((me ^ (token ^ column)) * 128, 128)
            out_ref[:, pl.ds(at, 128)] = part_ref[:, n * 128 : (n + 1) * 128]


def gather_rows(me, grad_refs, rows_ref):
    for rx, ref in enumerate(grad_refs):
        for rz in range(2):
            for k in range(4):
                at = pl.multiple_of(k * 128 + (me ^ (2 * rx + rz)) * 16, 16)
                rows_ref[pl.ds(at, 16), :] = ref[rz, k]


def weight_grad_kernel(scale, place_ref, *refs):
    grad_refs, hidden_refs, (near_ref, far_ref), rows_ref = refs[:4], refs[4:8], refs[8:10], refs[10]

    @pl.when(pl.program_id(0) == 0)
    def _():
        gather_rows(place_ref[0], grad_refs, rows_ref)

    hidden = jnp.concatenate([ref[...] for ref in hidden_refs], axis=0)
    product = lax.dot_general(
        hidden, rows_ref[...], (((0,), (0,)), ((), ())), preferred_element_type=F32
    )
    product = (product * scale).astype(BF16)
    for n in range(4):
        near_ref[n] = product[:, n * 128 : (n + 1) * 128]
        far_ref[n] = product[:, (n + 4) * 128 : (n + 5) * 128]


def token_kernel(place_ref, *refs):
    grad_refs, hidden_refs, weight_refs = refs[:4], refs[4:8], refs[8:16]
    near_ref, far_ref = refs[16:18]
    out_refs, rows_ref, total_ref = refs[18:22], refs[22], refs[23]
    step = pl.program_id(0)
    me = place_ref[0]

    @pl.when(step == 0)
    def _():
        gather_rows(me, grad_refs, rows_ref)

    hidden = jnp.concatenate([ref[...] for ref in hidden_refs], axis=0)
    weight = jnp.concatenate([ref[...] for ref in weight_refs], axis=1)
    back = lax.dot_general(
        rows_ref[...], weight, (((1,), (1,)), ((), ())), preferred_element_type=F32
    ).astype(BF16)
    for n, (ref, at) in enumerate(((near_ref, 0), (far_ref, 0), (near_ref, 1), (far_ref, 1))):
        ref[at] = back[n * 128 : (n + 1) * 128]
    part = jnp.dot(hidden, weight, preferred_element_type=F32)

    @pl.when(step == 0)
    def _():
        total_ref[...] = part

    @pl.when(step > 0)
    def _():
        total_ref[...] += part

    @pl.when(step == pl.num_programs(0) - 1)
    def _():
        for rx, ref in enumerate(out_refs):
            for rz in range(2):
                for k in range(4):
                    at = pl.multiple_of(k * 128 + (me ^ (2 * rx + rz)) * 16, 16)
                    ref[rz, k] = total_ref[pl.ds(at, 16), :].astype(BF16)


def add(*arrays):
    total = arrays[0].astype(F32)
    for array in arrays[1:]:
        total = total + array.astype(F32)
    return total


def on_device(preactivation, keep_codes, down_weight, output_grad):
    rows, width = preactivation.shape
    scale = 1.0 / math.sqrt(rows * lax.axis_size("dp"))
    dp_place, mp_place = place("dp"), place("mp")
    shape = jax.ShapeDtypeStruct
    piece = shape((rows, width), BF16)

    grad_parts = call(
        split_kernel,
        [shape((16, 1024), BF16)] * 4,
        in_specs=[in_smem(), whole()],
        out_specs=[whole()] * 4,
        moved=2 * 131072,
    )(dp_place, output_grad)
    grad_parts = [grad_parts[0]] + [dp_swap(p, k) for p, k in zip(grad_parts[1:], TOKEN_PARTS[1:])]
    grad_own = jnp.stack(grad_parts)
    grad_pair = jnp.stack([grad_own, mp_swap(grad_own, 1)])
    grads = [grad_pair] + [mp_swap(grad_pair, 2 * rx) for rx in (1, 2, 3)]

    weight_z = dp_swap(down_weight, COLS_Z)
    weight_y = dp_swap(down_weight, COLS_Y)
    weight_yz = dp_swap(weight_z, COLS_Y)
    weights = [down_weight, weight_y, weight_z, weight_yz]
    weights = weights + [dp_swap(w, CORE) for w in weights]

    hidden, slope = call(
        mask_kernel,
        [piece, piece],
        in_specs=[whole()] * 2,
        out_specs=[whole()] * 2,
        flops=2 * rows * 448 * 512,
        moved=3 * 458752 + 229376,
    )(preactivation, keep_codes)
    hidden_z = dp_swap(hidden, ROWS_Z)
    hidden_y = dp_swap(hidden, ROWS_Y)
    hidden_yz = dp_swap(hidden_z, ROWS_Y)
    hiddens = [hidden, hidden_y, hidden_z, hidden_yz]

    grad_spec = pl.BlockSpec((2, 4, 16, 1024), lambda f: (0, 0, 0, 0))
    hidden_spec = pl.BlockSpec((rows, STEP), lambda f: (0, f))
    weight_spec = pl.BlockSpec((STEP, 128), lambda f: (f, 0))
    near, far = call(
        lambda *refs: weight_grad_kernel(scale, *refs),
        [shape((4, width, 128), BF16)] * 2,
        grid=(width // STEP,),
        in_specs=[in_smem()] + [grad_spec] * 4 + [hidden_spec] * 4,
        out_specs=[pl.BlockSpec((4, STEP, 128), lambda f: (0, f, 0))] * 2,
        scratch=[pltpu.VMEM((512, 1024), BF16)],
        flops=2 * 512 * 1024 * width,
        moved=6 * 2**20,
    )(mp_place, *grads, *hiddens)
    arrived = dp_swap(far, CORE)
    send = add(near[1::2], arrived[1::2]).astype(BF16)
    arrived_y = dp_swap(send, COLS_Y)
    send = add(near[2], arrived[2], arrived_y[1]).astype(BF16)
    weight_grad = add(near[0], arrived[0], arrived_y[0], dp_swap(send, COLS_Z)).astype(BF16)

    outs = call(
        token_kernel,
        [shape((2, rows, width), BF16)] * 2 + [shape((2, 4, 16, 1024), BF16)] * 4,
        grid=(width // STEP,),
        in_specs=[in_smem()] + [grad_spec] * 4 + [hidden_spec] * 4 + [weight_spec] * 8,
        out_specs=[pl.BlockSpec((2, rows, STEP), lambda f: (0, 0, f))] * 2 + [grad_spec] * 4,
        scratch=[pltpu.VMEM((512, 1024), BF16), pltpu.VMEM((512, 1024), F32)],
        flops=4 * 512 * 1024 * width,
        moved=9 * 2**20,
    )(mp_place, *grads, *hiddens, *weights)
    near, far, parts = outs[0], outs[1], outs[2:]
    arrived = dp_swap(far, ROWS_Y)
    send = add(near[1], arrived[1]).astype(BF16)
    back = add(near[0], arrived[0], dp_swap(send, ROWS_Z))
    input_grad = (slope.astype(F32) * back).astype(BF16)

    parts = [parts[0]] + [mp_swap(p, 2 * rx) for rx, p in zip((1, 2, 3), parts[1:])]
    pair = add(*parts)
    total = add(pair[0], mp_swap(pair[1].astype(BF16), 1)).astype(BF16)
    pieces = [total[0]] + [dp_swap(total[n], k) for n, k in enumerate(TOKEN_PARTS) if n]
    output = call(
        join_kernel,
        shape((16, 4096), BF16),
        in_specs=[in_smem()] + [whole()] * 4,
        out_specs=whole(),
        moved=2 * 131072,
    )(dp_place, *pieces)
    return (output, weight_grad, input_grad)


def solution(mesh):
    in_specs = (P("dp", "mp"), P("dp", "mp"), P("mp", "dp"), P(("dp", "mp"), None))
    out_specs = (P(("dp", "mp"), None), P("mp", "dp"), P("dp", "mp"))
    return jax.shard_map(
        on_device, mesh=mesh, in_specs=in_specs, out_specs=out_specs, check_vma=False
    )
```

```python
import math

import jax
import jax.numpy as jnp
from jax import lax
from jax.experimental import pallas as pl
from jax.experimental.pallas import tpu as pltpu
from jax.sharding import PartitionSpec as P

BF16 = jnp.bfloat16
F32 = jnp.float32

CORE = 1
ROWS_Y, ROWS_Z = 2, 16
COLS_Y, COLS_Z = 6, 8
TOKEN_PARTS = (0, ROWS_Y, ROWS_Z, ROWS_Y ^ ROWS_Z)
COLUMN_PARTS = (0, COLS_Y, COLS_Z, COLS_Y ^ COLS_Z)
COLUMN_BLOCKS = COLUMN_PARTS + tuple(k ^ CORE for k in COLUMN_PARTS)
STEP = 256
COST = 1
EARLY = 64


def swap(array, axis, size, k):
    return lax.ppermute(array, axis, [(i, i ^ k) for i in range(size)])


def dp_swap(array, k):
    return swap(array, "dp", 32, k)


def mp_swap(array, k):
    return swap(array, "mp", 8, k)


def place(axis):
    return jnp.reshape(lax.axis_index(axis).astype(jnp.int32), (1,))


def in_smem():
    return pl.BlockSpec(memory_space=pltpu.SMEM)


def whole():
    return pl.BlockSpec(memory_space=pltpu.VMEM)


def call(kernel, out_shape, scratch=(), grid=None, in_specs=None, out_specs=None, flops=0, moved=0, limit=16 * 2**20):
    return pl.pallas_call(
        kernel,
        out_shape=out_shape,
        grid=grid or (),
        in_specs=in_specs,
        out_specs=out_specs,
        scratch_shapes=list(scratch),
        compiler_params=pltpu.CompilerParams(vmem_limit_bytes=limit),
        cost_estimate=pl.CostEstimate(flops=flops, bytes_accessed=moved, transcendentals=0),
    )


def mask_kernel(pre_in, code_in, hidden_ref, slope_ref, pre_ref, code_ref, sems):
    copies = [
        pltpu.make_async_copy(pre_in, pre_ref, sems.at[0]),
        pltpu.make_async_copy(code_in, code_ref, sems.at[1]),
    ]
    for copy in copies:
        copy.start()
    for copy in copies:
        copy.wait()
    groups = code_ref.shape[0]
    for at in range(0, groups, 128):
        size = min(128, groups - at)
        spread = (
            lax.broadcasted_iota(jnp.int32, (size, 4 * size), 1) // 4
            == lax.broadcasted_iota(jnp.int32, (size, 4 * size), 0)
        ).astype(BF16)
        codes = code_ref[at : at + size, :].astype(F32).astype(BF16)
        code = lax.dot_general(
            codes, spread, (((0,), (0,)), ((), ())), preferred_element_type=F32
        )
        lane = lax.broadcasted_iota(jnp.int32, code.shape, 1) % 4
        kept = (
            ((lane == 0) & (code < 2.5))
            | ((lane == 1) & ((code == 0.0) | (code == 3.0) | (code == 4.0)))
            | ((lane == 2) & ((code == 1.0) | (code == 3.0) | (code == 5.0)))
            | ((lane == 3) & ((code == 2.0) | (code > 3.5)))
        )
        columns = slice(4 * at, 4 * (at + size))
        positive = jnp.where(kept, jnp.maximum(pre_ref[:, columns].astype(F32), 0.0), 0.0)
        hidden_ref[:, columns] = (positive * positive).astype(BF16)
        slope_ref[:, columns] = (2.0 * positive).astype(BF16)


def first_kernel(place_ref, grad_ref, grad_far, hidden_ref, weight_ref, *refs):
    part_refs, half_ref, weight_out = refs[-6:-2], refs[-2], refs[-1]
    me = place_ref[0]
    for out_ref, token in zip(part_refs, TOKEN_PARTS):
        for n, column in enumerate(COLUMN_BLOCKS):
            at = pl.ds(pl.multiple_of((me ^ (token ^ column)) * 128, 128), 128)
            out_ref[0, :, n * 128 : (n + 1) * 128] = grad_ref[:, at]
            out_ref[1, :, n * 128 : (n + 1) * 128] = grad_far[:, at]
    half_ref[...] = hidden_ref[: half_ref.shape[0]]
    weight_out[...] = weight_ref[...]


def second_kernel(*refs):
    part_refs, hidden_ref, weight_z = refs[:4], refs[4], refs[5]
    near_ref, far_ref, half_ref, hidden_out, weight_out = refs[-5:]
    for n, ref in enumerate(part_refs):
        near_ref[n] = ref[0]
        far_ref[n] = ref[1]
    half_ref[...] = hidden_ref[half_ref.shape[0] :]
    hidden_out[...] = hidden_ref[...]
    weight_out[...] = weight_z[...]


def third_kernel(near_ref, near_x, far_ref, far_x, z0_ref, z1_ref, *refs):
    weight_refs = refs[:4]
    near_out, far_out, hidden_z, weights = refs[-4:]
    near_out[0] = near_ref[...]
    near_out[1] = near_x[...]
    far_out[0] = far_ref[...]
    far_out[1] = far_x[...]
    hidden_z[:64] = z0_ref[...]
    hidden_z[64:] = z1_ref[...]
    for n, ref in enumerate(weight_refs):
        weights[n] = ref[...]


def gather_rows(me, grad_refs, rows_ref):
    near_two, near_rest, far_two, far_rest = grad_refs
    for k in range(4):
        for rx, ref in enumerate((near_two.at[0], near_two.at[1], near_rest.at[1], near_rest.at[0])):
            rows_ref[part_at(me, rx, 0, k), :] = ref[k]
        for rx, ref in enumerate((far_two.at[0], far_rest.at[0], far_rest.at[1], far_two.at[1])):
            rows_ref[part_at(me, rx, 1, k), :] = ref[k]


def part_at(me, rx, rz, k):
    return pl.ds(pl.multiple_of(k * 128 + (me ^ (2 * rx + rz)) * 16, 16), 16)


def steps(width, body):
    for at in range(0, width, STEP):
        body(slice(at, at + STEP))


def output_kernel(place_ref, *refs):
    hidden_refs, (mine_ref, far_ref) = refs[:4], refs[4:6]
    first0, first3, first_send, second0, second1, second_send, rows_ref = refs[6:]
    hidden = jnp.concatenate([ref[...] for ref in hidden_refs], axis=0)
    for n in range(4):
        ref = (mine_ref, far_ref)[n // 2]
        weight = jnp.concatenate([ref[2 * n % 4], ref[2 * n % 4 + 1]], axis=1)
        total = jnp.dot(hidden, weight, preferred_element_type=F32).astype(BF16)
        rows_ref[:, 256 * n : 256 * (n + 1)] = total
    me = place_ref[0]
    for k in range(4):
        for rx, ref in enumerate((first0, first_send.at[0], first_send.at[1], first3)):
            ref[k] = rows_ref[part_at(me, rx, 0, k), :]
        for rx, ref in enumerate((second0, second1, second_send.at[1], second_send.at[0])):
            ref[k] = rows_ref[part_at(me, rx, 1, k), :]


def weight_grad_kernel(scale, place_ref, *refs):
    grad_refs, hidden_refs, (near_ref, away_ref, rows_ref) = refs[:4], refs[4:8], refs[-3:]
    gather_rows(place_ref[0], grad_refs, rows_ref)

    def body(at):
        hidden = jnp.concatenate([ref[:, at] for ref in hidden_refs], axis=0)
        product = lax.dot_general(
            hidden, rows_ref[...], (((0,), (0,)), ((), ())), preferred_element_type=F32
        )
        product = (product * scale).astype(BF16)
        for n in range(4):
            near_ref[n, at, :] = product[:, n * 128 : (n + 1) * 128]
            away_ref[n, at, :] = product[:, (n + 4) * 128 : (n + 5) * 128]

    steps(near_ref.shape[1], body)


def back_kernel(rows_ref, mine_ref, far_ref, *refs):
    near_ref, half0_ref, half1_ref = refs[-3:]
    middle = half0_ref.shape[1]

    def body(at):
        weight = jnp.concatenate([ref[n, at, :] for ref in (mine_ref, far_ref) for n in range(4)], axis=1)
        back = lax.dot_general(
            rows_ref[...], weight, (((1,), (1,)), ((), ())), preferred_element_type=F32
        ).astype(BF16)
        for n in range(2):
            near_ref[n, :, at] = back[256 * n : 256 * n + 128]
            half0_ref[n, :, at] = back[256 * n + 128 : 256 * n + 128 + middle]
            half1_ref[n, :, at] = back[256 * n + 128 + middle : 256 * n + 256]

    steps(mine_ref.shape[1], body)


def added(*arrays):
    total = arrays[0].astype(F32)
    for array in arrays[1:]:
        total = total + array.astype(F32)
    return total


def y_kernel(near_ref, far_ref, half0_ref, *refs):
    first0, first3, first_far, second0, second1, second_far = refs[:6]
    send0_ref, send1_ref, sum_ref, half0_out, first_sum, first_send, second_sum, second_send = refs[6:]
    half0_out[...] = half0_ref[...]
    first_sum[...] = added(first0[...], first_far[0])
    first_send[...] = added(first3[...], first_far[1]).astype(BF16)
    second_sum[...] = added(second0[...], second_far[0])
    second_send[...] = added(second1[...], second_far[1]).astype(BF16)
    middle = send0_ref.shape[1]
    for n in range(2):
        send = added(near_ref[2 * n + 1], far_ref[2 * n + 1]).astype(BF16)
        send0_ref[n] = send[:middle]
        send1_ref[n] = send[middle:]
        sum_ref[n] = added(near_ref[2 * n], far_ref[2 * n])


def z0_kernel(sum_ref, far0_ref, back_ref, back0_ref, first_ref, first_far, second_ref, *refs):
    weight1_ref, back1_ref = refs[:2]
    weight_out, back_out, weight1_out, back1_out, total_ref, send_ref = refs[2:]
    middle = far0_ref.shape[1]
    weight_out[...] = added(sum_ref[1, :middle], far0_ref[1]).astype(BF16)
    back_out[...] = added(back_ref[1, : back0_ref.shape[1]], back0_ref[1]).astype(BF16)
    weight1_out[...] = weight1_ref[...]
    back1_out[...] = back1_ref[...]
    total = added(first_ref[...], first_far[...], second_ref[...]).astype(BF16)
    total_ref[...] = total
    send_ref[0] = total[1]
    send_ref[1] = total[3]


def z1_kernel(sum_ref, far1_ref, back_ref, back1_ref, total_ref, arrived_ref, *refs):
    weight_out, back_out, send_ref = refs[-3:]
    middle = sum_ref.shape[1] - far1_ref.shape[1]
    weight_out[...] = added(sum_ref[1, middle:], far1_ref[1]).astype(BF16)
    middle = back_ref.shape[1] - back1_ref.shape[1]
    back_out[...] = added(back_ref[1, middle:], back1_ref[1]).astype(BF16)
    send_ref[0] = total_ref[2]
    send_ref[1] = arrived_ref[1]


def last_kernel(place_ref, *refs):
    sum_ref, far0, far1, z0, z1, back_ref, back0, back1, backz0, backz1, slope_ref = refs[:11]
    total_ref, arrived_y, arrived_z, weight_out, input_out, output_ref = refs[11:]
    middle = far0.shape[1]
    for at, far, last in ((slice(0, middle), far0, z0), (slice(middle, None), far1, z1)):
        weight_out[at] = added(sum_ref[0, at], far[0], last[...]).astype(BF16)
    middle = back0.shape[1]
    for at, far, last in ((slice(0, middle), back0, backz0), (slice(middle, None), back1, backz1)):
        back = added(back_ref[0, at], far[0], last[...])
        input_out[at] = (slope_ref[at].astype(F32) * back).astype(BF16)
    me = place_ref[0]
    parts = (total_ref.at[0], arrived_y.at[0], arrived_z.at[0], arrived_z.at[1])
    for part_ref, token in zip(parts, TOKEN_PARTS):
        for n, column in enumerate(COLUMN_BLOCKS):
            at = pl.multiple_of((me ^ (token ^ column)) * 128, 128)
            output_ref[:, pl.ds(at, 128)] = part_ref[:, n * 128 : (n + 1) * 128]


def move(kernel, out_shape, *arrays, scratch=(), flops=COST):
    return call(
        kernel,
        out_shape,
        in_specs=[in_smem() if a.dtype == jnp.int32 and a.size == 1 else whole() for a in arrays],
        out_specs=[whole()] * len(out_shape),
        scratch=scratch,
        flops=flops,
        moved=COST,
    )(*arrays)


def on_device(preactivation, keep_codes, down_weight, output_grad):
    rows, width = preactivation.shape
    scale = 1.0 / math.sqrt(rows * lax.axis_size("dp"))
    dp_place, mp_place = place("dp"), place("mp")

    def shape(*sizes):
        return jax.ShapeDtypeStruct(sizes, BF16)

    def wide(*sizes):
        return jax.ShapeDtypeStruct(sizes, F32)

    piece, half, column = shape(rows, width), shape(rows // 2, width), shape(width, 128)
    part, pair = shape(4, 16, 1024), shape(2, 4, 16, 1024)
    early = width * EARLY // rows
    split0, split1 = shape(2, early, 128), shape(2, width - early, 128)
    rows_scratch = [pltpu.VMEM((512, 1024), BF16)]

    grad_far = mp_swap(output_grad, 1)
    codes = keep_codes.T
    hidden, slope = call(
        mask_kernel,
        [piece, piece],
        in_specs=[pl.BlockSpec(memory_space=pl.ANY)] * 2,
        out_specs=[whole()] * 2,
        scratch=[
            pltpu.VMEM(preactivation.shape, BF16),
            pltpu.VMEM(codes.shape, jnp.int32),
            pltpu.SemaphoreType.DMA((2,)),
        ],
        flops=10**11,
    )(preactivation, codes)
    outs = move(
        first_kernel,
        [shape(2, 16, 1024)] * 4 + [half, column],
        dp_place,
        output_grad,
        grad_far,
        hidden,
        down_weight,
    )
    parts, half_out, weight_out = outs[:4], outs[4], outs[5]

    parts = [parts[0]] + [dp_swap(p, k) for p, k in zip(parts[1:], TOKEN_PARTS[1:])]
    weight_z = dp_swap(weight_out, COLS_Z)
    weight_y = dp_swap(weight_out, COLS_Y)
    hidden_z0 = dp_swap(half_out, ROWS_Z)
    near, far, half_out, hidden_out, weight_out = move(
        second_kernel, [part, part, half, piece, column], *parts, hidden, weight_z, hidden_z0, weight_y
    )

    near_x = mp_swap(near, 2)
    far_x = mp_swap(far, 6)
    hidden_z1 = dp_swap(half_out, ROWS_Z)
    hidden_y = dp_swap(hidden_out, ROWS_Y)
    weight_yz = dp_swap(weight_out, COLS_Y)
    near_two, far_two, hidden_z, weights = move(
        third_kernel,
        [pair, pair, piece, shape(4, width, 128)],
        near,
        near_x,
        far,
        far_x,
        hidden_z0,
        hidden_z1,
        down_weight,
        weight_y,
        weight_z,
        weight_yz,
        hidden_y,
    )

    near_rest = mp_swap(near_two, 6)
    far_rest = mp_swap(far_two, 2)
    hidden_yz = dp_swap(hidden_z, ROWS_Y)
    weights_far = dp_swap(weights, CORE)
    grads = [near_two, near_rest, far_two, far_rest]
    hiddens = [hidden, hidden_y, hidden_z, hidden_yz]

    first0, first3, first_send, second0, second1, second_send = move(
        output_kernel,
        [part, part, pair, part, part, pair],
        mp_place,
        *hiddens,
        weights,
        weights_far,
        scratch=rows_scratch,
    )
    first_far = mp_swap(first_send, 2)
    second_far = mp_swap(second_send, 6)
    near, away, grad_rows = move(
        lambda *refs: weight_grad_kernel(scale, *refs),
        [shape(4, width, 128)] * 2 + [shape(512, 1024)],
        mp_place,
        *grads,
        *hiddens,
        first0,
        flops=5 * 10**9,
    )
    away = dp_swap(away, CORE)
    back_near, half0, half1 = move(
        back_kernel,
        [shape(2, rows, width), shape(2, EARLY, width), shape(2, rows - EARLY, width)],
        grad_rows,
        weights,
        weights_far,
        flops=5 * 10**9,
    )

    send0, send1, sums, half0, first, first_send, second, second_send = move(
        y_kernel,
        [split0, split1, wide(2, width, 128), shape(2, EARLY, width)]
        + [wide(4, 16, 1024), part] * 2,
        near,
        away,
        half0,
        first0,
        first3,
        first_far,
        second0,
        second1,
        second_far,
    )
    far0 = dp_swap(send0, COLS_Y)
    back0 = dp_swap(half0, ROWS_Y)
    first_far = mp_swap(first_send, 6)
    second = mp_swap(added(second, mp_swap(second_send, 2)).astype(BF16), 1)

    weight_z0, back_z0, send1, half1, total, total_send = move(
        z0_kernel,
        [
            shape(early, 128),
            shape(EARLY, width),
            split1,
            shape(2, rows - EARLY, width),
            part,
            shape(2, 16, 1024),
        ],
        sums,
        far0,
        back_near,
        back0,
        first,
        first_far,
        second,
        send1,
        half1,
    )
    weight_z0 = dp_swap(weight_z0, COLS_Z)
    back_z0 = dp_swap(back_z0, ROWS_Z)
    far1 = dp_swap(send1, COLS_Y)
    back1 = dp_swap(half1, ROWS_Y)
    arrived_y = dp_swap(total_send, ROWS_Y)

    weight_z1, back_z1, total_send = move(
        z1_kernel,
        [shape(width - early, 128), shape(rows - EARLY, width), shape(2, 16, 1024)],
        sums,
        far1,
        back_near,
        back1,
        total,
        arrived_y,
        weight_z0,
        back_z0,
    )
    weight_z1 = dp_swap(weight_z1, COLS_Z)
    back_z1 = dp_swap(back_z1, ROWS_Z)
    arrived_z = dp_swap(total_send, ROWS_Z)
    weight_grad, input_grad, output = move(
        last_kernel,
        [column, piece, shape(16, 4096)],
        dp_place,
        sums,
        far0,
        far1,
        weight_z0,
        weight_z1,
        back_near,
        back0,
        back1,
        back_z0,
        back_z1,
        slope,
        total,
        arrived_y,
        arrived_z,
    )
    return (output, weight_grad, input_grad)


def solution(mesh):
    in_specs = (P("dp", "mp"), P("dp", "mp"), P("mp", "dp"), P(("dp", "mp"), None))
    out_specs = (P(("dp", "mp"), None), P("mp", "dp"), P("dp", "mp"))
    return jax.shard_map(
        on_device, mesh=mesh, in_specs=in_specs, out_specs=out_specs, check_vma=False
    )
```

```python
import math

import jax
import jax.numpy as jnp
from jax import lax
from jax.experimental import pallas as pl
from jax.experimental.pallas import tpu as pltpu
from jax.sharding import PartitionSpec as P

BF16 = jnp.bfloat16
F32 = jnp.float32

CORE = 1
ROWS_Y, ROWS_Z = 2, 16
COLS_Y, COLS_Z = 6, 8
TOKEN_PARTS = (0, ROWS_Y, ROWS_Z, ROWS_Y ^ ROWS_Z)
COLUMN_PARTS = (0, COLS_Y, COLS_Z, COLS_Y ^ COLS_Z)
COLUMN_BLOCKS = COLUMN_PARTS + tuple(k ^ CORE for k in COLUMN_PARTS)
STEP = 256
COST = 1
PACKED = 3 * 384 + 256
KEPT = 3 * 256 + 128
CHUNKS = ((0, 512, 0, 0), (512, 1024, 384, 256), (1024, 1536, 768, 512), (1536, 1792, 1152, 768))
EARLY = 80


def swap(array, axis, size, k):
    return lax.ppermute(array, axis, [(i, i ^ k) for i in range(size)])


def dp_swap(array, k):
    return swap(array, "dp", 32, k)


def mp_swap(array, k):
    return swap(array, "mp", 8, k)


def place(axis):
    return jnp.reshape(lax.axis_index(axis).astype(jnp.int32), (1,))


def in_smem():
    return pl.BlockSpec(memory_space=pltpu.SMEM)


def whole():
    return pl.BlockSpec(memory_space=pltpu.VMEM)


def call(kernel, out_shape, scratch=(), grid=None, in_specs=None, out_specs=None, flops=0, moved=0, limit=12 * 2**20):
    return pl.pallas_call(
        kernel,
        out_shape=out_shape,
        grid=grid or (),
        in_specs=in_specs,
        out_specs=out_specs,
        scratch_shapes=list(scratch),
        compiler_params=pltpu.CompilerParams(vmem_limit_bytes=limit),
        cost_estimate=pl.CostEstimate(flops=flops, bytes_accessed=moved, transcendentals=0),
    )


def spread(rows, width, start=0):
    of = lax.broadcasted_iota(jnp.int32, (rows, width), 1) // 4 + start
    return (of == lax.broadcasted_iota(jnp.int32, (rows, width), 0)).astype(BF16)


def spreads(width):
    if width == 512:
        return spread(128, 512), spread(128, 512)
    return spread(128, 256), spread(128, 256, 64)


def matmul(a, b):
    return jnp.dot(a, b, preferred_element_type=F32)


def matmul_t(a, b):
    return lax.dot_general(a, b, (((1,), (1,)), ((), ())), preferred_element_type=F32)


def kept_places(code):
    first = (code > 2.5).astype(F32) + (code > 4.5).astype(F32)
    second = 3.0 - ((code == 1.0) | (code == 3.0)).astype(F32) - 2.0 * (code == 0.0).astype(F32)
    return first.astype(BF16), second.astype(BF16)


def lanes(shape):
    return (lax.broadcasted_iota(jnp.int32, shape, 1) % 4).astype(F32)


def put_kept(ref, at, kept0, kept1, width):
    to0, to1 = spreads(width)
    if width == 512:
        ref[:, at : at + 128] = matmul_t(kept0, to0).astype(BF16)
        ref[:, at + 128 : at + 256] = matmul_t(kept1, to1).astype(BF16)
    else:
        ref[:, at : at + 128] = (matmul_t(kept0, to0) + matmul_t(kept1, to1)).astype(BF16)


def mask_kernel(pre_ref, code_ref, hidden_ref, slope_ref, first_ref, packed_ref):
    for low, high, at, _ in CHUNKS:
        width = high - low
        code = code_ref[low // 4 : high // 4, :].astype(F32)
        first, second = kept_places(code)
        turn = (((0,), (0,)), ((), ()))
        to = spread(width // 4, width)
        first = lax.dot_general(first, to, turn, preferred_element_type=F32)
        second = lax.dot_general(second, to, turn, preferred_element_type=F32)
        lane = lanes(first.shape)
        is_first, is_second = first == lane, second == lane
        positive = jnp.maximum(pre_ref[:, low:high].astype(F32), 0.0)
        square = positive * positive
        kept0 = jnp.where(is_first, square, 0.0)
        kept1 = jnp.where(is_second, square, 0.0)
        hidden_ref[:, low:high] = (kept0 + kept1).astype(BF16)
        slope_ref[:, low:high] = jnp.where(is_first | is_second, 2.0 * positive, 0.0).astype(BF16)
        first_ref[:, low:high] = jnp.where(is_first, 1.0, 0.0).astype(BF16)
        put_kept(packed_ref, at, kept0.astype(BF16), kept1.astype(BF16), width)
        same = lax.broadcasted_iota(jnp.int32, (width // 4, 128), 0)
        same = (same == lax.broadcasted_iota(jnp.int32, same.shape, 1)).astype(BF16)
        codes = lax.dot_general(code.astype(BF16), same, turn, preferred_element_type=F32)
        at = at + (256 if width == 512 else 128)
        packed_ref[:, at : at + 128] = codes.astype(BF16)


def spread_kept(ref, at, width):
    to0, to1 = spreads(width)
    values = ref[:, at : at + 128]
    others = ref[:, at + 128 : at + 256] if width == 512 else values
    return matmul(values, to0), matmul(others, to1)


def unpack_kernel(*refs):
    count = len(refs) // 4
    for n in range(count):
        packed_ref = refs[n]
        hidden_ref, first_ref, second_ref = refs[count + 3 * n : count + 3 * n + 3]
        for low, high, at, _ in CHUNKS:
            width = high - low
            value0, value1 = spread_kept(packed_ref, at, width)
            at = at + (256 if width == 512 else 128)
            first, second = kept_places(packed_ref[:, at : at + 128].astype(F32))
            to = spreads(width)[0]
            first, second = matmul(first, to), matmul(second, to)
            lane = lanes(first.shape)
            is_first, is_second = first == lane, second == lane
            hidden = jnp.where(is_first, value0, jnp.where(is_second, value1, 0.0))
            hidden_ref[:, low:high] = hidden.astype(BF16)
            first_ref[:, low:high] = jnp.where(is_first, 1.0, 0.0).astype(BF16)
            second_ref[:, low:high] = jnp.where(is_second, 1.0, 0.0).astype(BF16)


def first_kernel(place_ref, grad_ref, grad_far, hidden_ref, weight_ref, *refs):
    part_refs, half_ref, weight_out = refs[-6:-2], refs[-2], refs[-1]
    me = place_ref[0]
    for out_ref, token in zip(part_refs, TOKEN_PARTS):
        for n, column in enumerate(COLUMN_BLOCKS):
            at = pl.ds(pl.multiple_of((me ^ (token ^ column)) * 128, 128), 128)
            out_ref[0, :, n * 128 : (n + 1) * 128] = grad_ref[:, at]
            out_ref[1, :, n * 128 : (n + 1) * 128] = grad_far[:, at]
    half_ref[...] = hidden_ref[: half_ref.shape[0]]
    weight_out[...] = weight_ref[...]


def second_kernel(*refs):
    part_refs, hidden_ref, weight_z = refs[:4], refs[4], refs[5]
    near_ref, far_ref, half_ref, hidden_out, weight_out = refs[-5:]
    for n, ref in enumerate(part_refs):
        near_ref[n] = ref[0]
        far_ref[n] = ref[1]
    half_ref[...] = hidden_ref[half_ref.shape[0] :]
    hidden_out[...] = hidden_ref[...]
    weight_out[...] = weight_z[...]


def third_kernel(near_ref, near_x, far_ref, far_x, z0_ref, z1_ref, *refs):
    weight_refs = refs[:4]
    near_out, far_out, hidden_z, weights = refs[-4:]
    near_out[0] = near_ref[...]
    near_out[1] = near_x[...]
    far_out[0] = far_ref[...]
    far_out[1] = far_x[...]
    hidden_z[:64] = z0_ref[...]
    hidden_z[64:] = z1_ref[...]
    for n, ref in enumerate(weight_refs):
        weights[n] = ref[...]


def gather_rows(me, grad_refs, rows_ref):
    near_two, near_rest, far_two, far_rest = grad_refs
    for k in range(4):
        for rx, ref in enumerate((near_two.at[0], near_two.at[1], near_rest.at[1], near_rest.at[0])):
            rows_ref[part_at(me, rx, 0, k), :] = ref[k]
        for rx, ref in enumerate((far_two.at[0], far_rest.at[0], far_rest.at[1], far_two.at[1])):
            rows_ref[part_at(me, rx, 1, k), :] = ref[k]


def part_at(me, rx, rz, k):
    return pl.ds(pl.multiple_of(k * 128 + (me ^ (2 * rx + rz)) * 16, 16), 16)


def steps(width, body):
    for at in range(0, width, STEP):
        body(slice(at, at + STEP))


def output_kernel(place_ref, *refs):
    hidden_refs, (mine_ref, far_ref) = refs[:4], refs[4:6]
    first0, first3, first_send, second0, second1, second_send, rows_ref = refs[6:]
    hidden = jnp.concatenate([ref[...] for ref in hidden_refs], axis=0)
    for n in range(4):
        ref = (mine_ref, far_ref)[n // 2]
        weight = jnp.concatenate([ref[2 * n % 4], ref[2 * n % 4 + 1]], axis=1)
        total = jnp.dot(hidden, weight, preferred_element_type=F32).astype(BF16)
        rows_ref[:, 256 * n : 256 * (n + 1)] = total
    me = place_ref[0]
    for k in range(4):
        for rx, ref in enumerate((first0, first_send.at[0], first_send.at[1], first3)):
            ref[k] = rows_ref[part_at(me, rx, 0, k), :]
        for rx, ref in enumerate((second0, second1, second_send.at[1], second_send.at[0])):
            ref[k] = rows_ref[part_at(me, rx, 1, k), :]


def weight_grad_kernel(scale, place_ref, *refs):
    grad_refs, hidden_refs, (near_ref, away_ref, rows_ref) = refs[:4], refs[4:8], refs[-3:]
    gather_rows(place_ref[0], grad_refs, rows_ref)

    def body(at):
        hidden = jnp.concatenate([ref[:, at] for ref in hidden_refs], axis=0)
        product = lax.dot_general(
            hidden, rows_ref[...], (((0,), (0,)), ((), ())), preferred_element_type=F32
        )
        product = (product * scale).astype(BF16)
        for n in range(4):
            near_ref[n, at, :] = product[:, n * 128 : (n + 1) * 128]
            away_ref[n, at, :] = product[:, (n + 4) * 128 : (n + 5) * 128]

    steps(near_ref.shape[1], body)


def back_kernel(rows_ref, mine_ref, far_ref, *refs):
    masks, (near_ref, z_ref, half0_ref, half1_ref, kept_ref) = refs[:6], refs[6:]
    for low, high, _, to in CHUNKS:
        at = slice(low, high)
        weight = jnp.concatenate([ref[n, at, :] for ref in (mine_ref, far_ref) for n in range(4)], axis=1)
        back = matmul_t(rows_ref[...], weight).astype(BF16)
        near_ref[:, at] = back[:128]
        first = jnp.concatenate([ref[:, at] for ref in masks[::2]], axis=0)
        second = jnp.concatenate([ref[:, at] for ref in masks[1::2]], axis=0)
        put_kept(kept_ref, to, back[128:] * first, back[128:] * second, high - low)
    middle = half0_ref.shape[1]
    z_ref[...] = kept_ref[128:256]
    for n in range(2):
        half0_ref[n] = kept_ref[256 * n : 256 * n + middle]
        half1_ref[n] = kept_ref[256 * n + middle : 256 * n + 128]


def added(*arrays):
    total = arrays[0].astype(F32)
    for array in arrays[1:]:
        total = total + array.astype(F32)
    return total


def y_kernel(near_ref, far_ref, half0_ref, *refs):
    first0, first3, first_far, second0, second1, second_far = refs[:6]
    send0_ref, send1_ref, sum_ref, half0_out, first_sum, first_send, second_sum, second_send = refs[6:]
    half0_out[...] = half0_ref[...]
    first_sum[...] = added(first0[...], first_far[0])
    first_send[...] = added(first3[...], first_far[1]).astype(BF16)
    second_sum[...] = added(second0[...], second_far[0])
    second_send[...] = added(second1[...], second_far[1]).astype(BF16)
    middle = send0_ref.shape[1]
    for n in range(2):
        send = added(near_ref[2 * n + 1], far_ref[2 * n + 1]).astype(BF16)
        send0_ref[n] = send[:middle]
        send1_ref[n] = send[middle:]
        sum_ref[n] = added(near_ref[2 * n], far_ref[2 * n])


def z0_kernel(sum_ref, far0_ref, back_ref, back0_ref, first_ref, first_far, second_ref, *refs):
    weight1_ref, back1_ref = refs[:2]
    weight_out, back_out, weight1_out, back1_out, total_ref, send_ref = refs[2:]
    middle = far0_ref.shape[1]
    weight_out[...] = added(sum_ref[1, :middle], far0_ref[1]).astype(BF16)
    back_out[...] = added(back_ref[: back0_ref.shape[1]], back0_ref[1]).astype(BF16)
    weight1_out[...] = weight1_ref[...]
    back1_out[...] = back1_ref[...]
    total = added(first_ref[...], first_far[...], second_ref[...]).astype(BF16)
    total_ref[...] = total
    send_ref[0] = total[1]
    send_ref[1] = total[3]


def z1_kernel(sum_ref, far1_ref, back_ref, back1_ref, total_ref, arrived_ref, *refs):
    weight_out, back_out, send_ref = refs[-3:]
    middle = sum_ref.shape[1] - far1_ref.shape[1]
    weight_out[...] = added(sum_ref[1, middle:], far1_ref[1]).astype(BF16)
    middle = back_ref.shape[0] - back1_ref.shape[1]
    back_out[...] = added(back_ref[middle:], back1_ref[1]).astype(BF16)
    send_ref[0] = total_ref[2]
    send_ref[1] = arrived_ref[1]


def last_kernel(place_ref, *refs):
    sum_ref, far0, far1, z0, z1, back_ref, back0, back1, backz0, backz1 = refs[:10]
    slope_ref, first_ref = refs[10:12]
    total_ref, arrived_y, arrived_z, weight_out, input_out, output_ref = refs[12:]
    middle = far0.shape[1]
    for at, far, last in ((slice(0, middle), far0, z0), (slice(middle, None), far1, z1)):
        weight_out[at] = added(sum_ref[0, at], far[0], last[...]).astype(BF16)
    middle = back0.shape[1]
    for at, far, last in ((slice(0, middle), back0.at[0], backz0), (slice(middle, None), back1.at[0], backz1)):
        for low, high, _, to in CHUNKS:
            far_0, far_1 = spread_kept(far, to, high - low)
            last_0, last_1 = spread_kept(last, to, high - low)
            arrived = jnp.where(first_ref[at, low:high].astype(F32) > 0.5, far_0 + last_0, far_1 + last_1)
            back = back_ref[at, low:high].astype(F32) + arrived
            input_out[at, low:high] = (slope_ref[at, low:high].astype(F32) * back).astype(BF16)
    me = place_ref[0]
    parts = (total_ref.at[0], arrived_y.at[0], arrived_z.at[0], arrived_z.at[1])
    for part_ref, token in zip(parts, TOKEN_PARTS):
        for n, column in enumerate(COLUMN_BLOCKS):
            at = pl.multiple_of((me ^ (token ^ column)) * 128, 128)
            output_ref[:, pl.ds(at, 128)] = part_ref[:, n * 128 : (n + 1) * 128]


def move(kernel, out_shape, *arrays, scratch=(), flops=COST):
    return call(
        kernel,
        out_shape,
        in_specs=[in_smem() if a.dtype == jnp.int32 and a.size == 1 else whole() for a in arrays],
        out_specs=[whole()] * len(out_shape),
        scratch=scratch,
        flops=flops,
        moved=COST,
    )(*arrays)


def on_device(preactivation, keep_codes, down_weight, output_grad):
    rows, width = preactivation.shape
    scale = 1.0 / math.sqrt(rows * lax.axis_size("dp"))
    dp_place, mp_place = place("dp"), place("mp")

    def shape(*sizes):
        return jax.ShapeDtypeStruct(sizes, BF16)

    def wide(*sizes):
        return jax.ShapeDtypeStruct(sizes, F32)

    piece, column = shape(rows, width), shape(width, 128)
    packed_shape, half = shape(rows, PACKED), shape(rows // 2, PACKED)
    part, pair = shape(4, 16, 1024), shape(2, 4, 16, 1024)
    early = width * EARLY // rows
    split0, split1 = shape(2, early, 128), shape(2, width - early, 128)
    rows_scratch = [pltpu.VMEM((512, 1024), BF16)]

    grad_far = mp_swap(output_grad, 1)
    hidden, slope, first_kept, packed = move(
        mask_kernel,
        [piece, piece, piece, packed_shape],
        preactivation,
        keep_codes.T,
        flops=10**11,
    )
    outs = move(
        first_kernel,
        [shape(2, 16, 1024)] * 4 + [half, column],
        dp_place,
        output_grad,
        grad_far,
        packed,
        down_weight,
    )
    parts, half_out, weight_out = outs[:4], outs[4], outs[5]

    parts = [parts[0]] + [dp_swap(p, k) for p, k in zip(parts[1:], TOKEN_PARTS[1:])]
    weight_z = dp_swap(weight_out, COLS_Z)
    weight_y = dp_swap(weight_out, COLS_Y)
    hidden_z0 = dp_swap(half_out, ROWS_Z)
    near, far, half_out, hidden_out, weight_out = move(
        second_kernel, [part, part, half, packed_shape, column], *parts, packed, weight_z, hidden_z0, weight_y
    )

    near_x = mp_swap(near, 2)
    far_x = mp_swap(far, 6)
    hidden_z1 = dp_swap(half_out, ROWS_Z)
    hidden_y = dp_swap(hidden_out, ROWS_Y)
    weight_yz = dp_swap(weight_out, COLS_Y)
    near_two, far_two, hidden_z, weights = move(
        third_kernel,
        [pair, pair, packed_shape, shape(4, width, 128)],
        near,
        near_x,
        far,
        far_x,
        hidden_z0,
        hidden_z1,
        down_weight,
        weight_y,
        weight_z,
        weight_yz,
        hidden_y,
    )

    near_rest = mp_swap(near_two, 6)
    far_rest = mp_swap(far_two, 2)
    hidden_yz = dp_swap(hidden_z, ROWS_Y)
    weights_far = dp_swap(weights, CORE)
    grads = [near_two, near_rest, far_two, far_rest]
    masked = [piece] * 3
    hidden_y, first_y, second_y, hidden_z, first_z, second_z = move(
        unpack_kernel, masked * 2, hidden_y, hidden_z, flops=3 * 10**9
    )
    hidden_yz, first_yz, second_yz = move(unpack_kernel, masked, hidden_yz)
    masks = [first_y, second_y, first_z, second_z, first_yz, second_yz]
    hiddens = [hidden, hidden_y, hidden_z, hidden_yz]

    first0, first3, first_send, second0, second1, second_send = move(
        output_kernel,
        [part, part, pair, part, part, pair],
        mp_place,
        *hiddens,
        weights,
        weights_far,
        scratch=rows_scratch,
    )
    first_far = mp_swap(first_send, 2)
    second_far = mp_swap(second_send, 6)
    near, away, grad_rows = move(
        lambda *refs: weight_grad_kernel(scale, *refs),
        [shape(4, width, 128)] * 2 + [shape(512, 1024)],
        mp_place,
        *grads,
        *hiddens,
        first0,
        flops=5 * 10**9,
    )
    away = dp_swap(away, CORE)
    back_near, back_z, half0, half1 = move(
        back_kernel,
        [piece, shape(rows, KEPT), shape(2, EARLY, KEPT), shape(2, rows - EARLY, KEPT)],
        grad_rows,
        weights,
        weights_far,
        *masks,
        scratch=[pltpu.VMEM((3 * rows, KEPT), BF16)],
        flops=5 * 10**9,
    )

    send0, send1, sums, half0, first, first_send, second, second_send = move(
        y_kernel,
        [split0, split1, wide(2, width, 128), shape(2, EARLY, KEPT)]
        + [wide(4, 16, 1024), part] * 2,
        near,
        away,
        half0,
        first0,
        first3,
        first_far,
        second0,
        second1,
        second_far,
    )
    far0 = dp_swap(send0, COLS_Y)
    back0 = dp_swap(half0, ROWS_Y)
    first_far = mp_swap(first_send, 6)
    second = mp_swap(added(second, mp_swap(second_send, 2)).astype(BF16), 1)

    weight_z0, back_z0, send1, half1, total, total_send = move(
        z0_kernel,
        [
            shape(early, 128),
            shape(EARLY, KEPT),
            split1,
            shape(2, rows - EARLY, KEPT),
            part,
            shape(2, 16, 1024),
        ],
        sums,
        far0,
        back_z,
        back0,
        first,
        first_far,
        second,
        send1,
        half1,
    )
    weight_z0 = dp_swap(weight_z0, COLS_Z)
    back_z0 = dp_swap(back_z0, ROWS_Z)
    far1 = dp_swap(send1, COLS_Y)
    back1 = dp_swap(half1, ROWS_Y)
    arrived_y = dp_swap(total_send, ROWS_Y)

    weight_z1, back_z1, total_send = move(
        z1_kernel,
        [shape(width - early, 128), shape(rows - EARLY, KEPT), shape(2, 16, 1024)],
        sums,
        far1,
        back_z,
        back1,
        total,
        arrived_y,
        weight_z0,
        back_z0,
    )
    weight_z1 = dp_swap(weight_z1, COLS_Z)
    back_z1 = dp_swap(back_z1, ROWS_Z)
    arrived_z = dp_swap(total_send, ROWS_Z)
    weight_grad, input_grad, output = move(
        last_kernel,
        [column, piece, shape(16, 4096)],
        dp_place,
        sums,
        far0,
        far1,
        weight_z0,
        weight_z1,
        back_near,
        back0,
        back1,
        back_z0,
        back_z1,
        slope,
        first_kept,
        total,
        arrived_y,
        arrived_z,
    )
    return (output, weight_grad, input_grad)


def solution(mesh):
    in_specs = (P("dp", "mp"), P("dp", "mp"), P("mp", "dp"), P(("dp", "mp"), None))
    out_specs = (P(("dp", "mp"), None), P("mp", "dp"), P("dp", "mp"))
    return jax.shard_map(
        on_device, mesh=mesh, in_specs=in_specs, out_specs=out_specs, check_vma=False
    )
```

```python
import math

import jax
import jax.numpy as jnp
from jax import lax
from jax.experimental import pallas as pl
from jax.experimental.pallas import tpu as pltpu
from jax.sharding import PartitionSpec as P

BF16 = jnp.bfloat16
F32 = jnp.float32

CORE = 1
ROWS_Y, ROWS_Z = 2, 16
COLS_Y, COLS_Z = 6, 8
TOKEN_PARTS = (0, ROWS_Y, ROWS_Z, ROWS_Y ^ ROWS_Z)
COLUMN_PARTS = (0, COLS_Y, COLS_Z, COLS_Y ^ COLS_Z)
COLUMN_BLOCKS = COLUMN_PARTS + tuple(k ^ CORE for k in COLUMN_PARTS)
STEP = 256
COST = 1
PACKED = 3 * 384 + 256
KEPT = 3 * 256 + 128
CHUNKS = ((0, 512, 0, 0), (512, 1024, 384, 256), (1024, 1536, 768, 512), (1536, 1792, 1152, 768))
EARLY = 64
FIRST = 48


def swap(array, axis, size, k):
    return lax.ppermute(array, axis, [(i, i ^ k) for i in range(size)])


def dp_swap(array, k):
    return swap(array, "dp", 32, k)


def mp_swap(array, k):
    return swap(array, "mp", 8, k)


def place(axis):
    return jnp.reshape(lax.axis_index(axis).astype(jnp.int32), (1,))


def in_smem():
    return pl.BlockSpec(memory_space=pltpu.SMEM)


def whole():
    return pl.BlockSpec(memory_space=pltpu.VMEM)


def call(kernel, out_shape, scratch=(), grid=None, in_specs=None, out_specs=None, flops=0, moved=0, limit=12 * 2**20):
    return pl.pallas_call(
        kernel,
        out_shape=out_shape,
        grid=grid or (),
        in_specs=in_specs,
        out_specs=out_specs,
        scratch_shapes=list(scratch),
        compiler_params=pltpu.CompilerParams(vmem_limit_bytes=limit),
        cost_estimate=pl.CostEstimate(flops=flops, bytes_accessed=moved, transcendentals=0),
    )


def spread(rows, width, start=0):
    of = lax.broadcasted_iota(jnp.int32, (rows, width), 1) // 4 + start
    return (of == lax.broadcasted_iota(jnp.int32, (rows, width), 0)).astype(BF16)


def spreads(width):
    if width == 512:
        return spread(128, 512), spread(128, 512)
    return spread(128, 256), spread(128, 256, 64)


def matmul(a, b):
    return jnp.dot(a, b, preferred_element_type=F32)


def matmul_t(a, b):
    return lax.dot_general(a, b, (((1,), (1,)), ((), ())), preferred_element_type=F32)


def kept_places(code):
    first = (code > 2.5).astype(F32) + (code > 4.5).astype(F32)
    second = 3.0 - ((code == 1.0) | (code == 3.0)).astype(F32) - 2.0 * (code == 0.0).astype(F32)
    return first.astype(BF16), second.astype(BF16)


def lanes(shape):
    return (lax.broadcasted_iota(jnp.int32, shape, 1) % 4).astype(F32)


def put_kept(ref, at, kept0, kept1, width):
    to0, to1 = spreads(width)
    if width == 512:
        ref[:, at : at + 128] = matmul_t(kept0, to0).astype(BF16)
        ref[:, at + 128 : at + 256] = matmul_t(kept1, to1).astype(BF16)
    else:
        ref[:, at : at + 128] = (matmul_t(kept0, to0) + matmul_t(kept1, to1)).astype(BF16)


def mask_kernel(pre_ref, code_ref, hidden_ref, slope_ref, first_ref, packed_ref):
    for low, high, at, _ in CHUNKS:
        width = high - low
        code = code_ref[low // 4 : high // 4, :].astype(F32)
        first, second = kept_places(code)
        turn = (((0,), (0,)), ((), ()))
        to = spread(width // 4, width)
        first = lax.dot_general(first, to, turn, preferred_element_type=F32)
        second = lax.dot_general(second, to, turn, preferred_element_type=F32)
        lane = lanes(first.shape)
        is_first, is_second = first == lane, second == lane
        positive = jnp.maximum(pre_ref[:, low:high].astype(F32), 0.0)
        square = positive * positive
        kept0 = jnp.where(is_first, square, 0.0)
        kept1 = jnp.where(is_second, square, 0.0)
        hidden_ref[:, low:high] = (kept0 + kept1).astype(BF16)
        slope_ref[:, low:high] = jnp.where(is_first | is_second, 2.0 * positive, 0.0).astype(BF16)
        first_ref[:, low:high] = jnp.where(is_first, 1.0, 0.0).astype(BF16)
        put_kept(packed_ref, at, kept0.astype(BF16), kept1.astype(BF16), width)
        same = lax.broadcasted_iota(jnp.int32, (width // 4, 128), 0)
        same = (same == lax.broadcasted_iota(jnp.int32, same.shape, 1)).astype(BF16)
        codes = lax.dot_general(code.astype(BF16), same, turn, preferred_element_type=F32)
        at = at + (256 if width == 512 else 128)
        packed_ref[:, at : at + 128] = codes.astype(BF16)


def spread_kept(ref, at, width):
    to0, to1 = spreads(width)
    values = ref[:, at : at + 128]
    others = ref[:, at + 128 : at + 256] if width == 512 else values
    return matmul(values, to0), matmul(others, to1)


def unpack_kernel(*refs):
    count = len(refs) // 4
    for n in range(count):
        packed_ref = refs[n]
        hidden_ref, first_ref, second_ref = refs[count + 3 * n : count + 3 * n + 3]
        for low, high, at, _ in CHUNKS:
            width = high - low
            value0, value1 = spread_kept(packed_ref, at, width)
            at = at + (256 if width == 512 else 128)
            first, second = kept_places(packed_ref[:, at : at + 128].astype(F32))
            to = spreads(width)[0]
            first, second = matmul(first, to), matmul(second, to)
            lane = lanes(first.shape)
            is_first, is_second = first == lane, second == lane
            hidden = jnp.where(is_first, value0, jnp.where(is_second, value1, 0.0))
            hidden_ref[:, low:high] = hidden.astype(BF16)
            first_ref[:, low:high] = jnp.where(is_first, 1.0, 0.0).astype(BF16)
            second_ref[:, low:high] = jnp.where(is_second, 1.0, 0.0).astype(BF16)


def first_kernel(place_ref, grad_ref, grad_far, hidden_ref, weight_ref, *refs):
    part_refs, half_ref, weight_out = refs[-6:-2], refs[-2], refs[-1]
    me = place_ref[0]
    for out_ref, token in zip(part_refs, TOKEN_PARTS):
        for n, column in enumerate(COLUMN_BLOCKS):
            at = pl.ds(pl.multiple_of((me ^ (token ^ column)) * 128, 128), 128)
            out_ref[0, :, n * 128 : (n + 1) * 128] = grad_ref[:, at]
            out_ref[1, :, n * 128 : (n + 1) * 128] = grad_far[:, at]
    half_ref[...] = hidden_ref[: half_ref.shape[0]]
    weight_out[...] = weight_ref[...]


def second_kernel(*refs):
    part_refs, hidden_ref, weight_z = refs[:4], refs[4], refs[5]
    near_ref, far_ref, half_ref, hidden_out, weight_out = refs[-5:]
    for n, ref in enumerate(part_refs):
        near_ref[n] = ref[0]
        far_ref[n] = ref[1]
    half_ref[...] = hidden_ref[hidden_ref.shape[0] - half_ref.shape[0] :]
    hidden_out[...] = hidden_ref[...]
    weight_out[...] = weight_z[...]


def third_kernel(near_ref, near_x, far_ref, far_x, z0_ref, z1_ref, *refs):
    weight_refs = refs[:4]
    near_out, far_out, hidden_z, weights = refs[-4:]
    near_out[0] = near_ref[...]
    near_out[1] = near_x[...]
    far_out[0] = far_ref[...]
    far_out[1] = far_x[...]
    hidden_z[: z0_ref.shape[0]] = z0_ref[...]
    hidden_z[z0_ref.shape[0] :] = z1_ref[...]
    for n, ref in enumerate(weight_refs):
        weights[n] = ref[...]


def gather_rows(me, grad_refs, rows_ref):
    near_two, near_rest, far_two, far_rest = grad_refs
    for k in range(4):
        for rx, ref in enumerate((near_two.at[0], near_two.at[1], near_rest.at[1], near_rest.at[0])):
            rows_ref[part_at(me, rx, 0, k), :] = ref[k]
        for rx, ref in enumerate((far_two.at[0], far_rest.at[0], far_rest.at[1], far_two.at[1])):
            rows_ref[part_at(me, rx, 1, k), :] = ref[k]


def part_at(me, rx, rz, k):
    return pl.ds(pl.multiple_of(k * 128 + (me ^ (2 * rx + rz)) * 16, 16), 16)


def steps(width, body):
    for at in range(0, width, STEP):
        body(slice(at, at + STEP))


def output_kernel(place_ref, *refs):
    hidden_refs, (mine_ref, far_ref) = refs[:4], refs[4:6]
    first0, first3, first_send, second0, second1, second_send, rows_ref = refs[-7:]
    hidden = jnp.concatenate([ref[...] for ref in hidden_refs], axis=0)
    for n in range(4):
        ref = (mine_ref, far_ref)[n // 2]
        weight = jnp.concatenate([ref[2 * n % 4], ref[2 * n % 4 + 1]], axis=1)
        total = jnp.dot(hidden, weight, preferred_element_type=F32).astype(BF16)
        rows_ref[:, 256 * n : 256 * (n + 1)] = total
    me = place_ref[0]
    for k in range(4):
        for rx, ref in enumerate((first0, first_send.at[0], first_send.at[1], first3)):
            ref[k] = rows_ref[part_at(me, rx, 0, k), :]
        for rx, ref in enumerate((second0, second1, second_send.at[1], second_send.at[0])):
            ref[k] = rows_ref[part_at(me, rx, 1, k), :]


def weight_grad_kernel(scale, place_ref, *refs):
    grad_refs, hidden_refs, (near_ref, away_ref, rows_ref) = refs[:4], refs[4:8], refs[-3:]
    gather_rows(place_ref[0], grad_refs, rows_ref)

    def body(at):
        hidden = jnp.concatenate([ref[:, at] for ref in hidden_refs], axis=0)
        product = lax.dot_general(
            hidden, rows_ref[...], (((0,), (0,)), ((), ())), preferred_element_type=F32
        )
        product = (product * scale).astype(BF16)
        for n in range(4):
            near_ref[n, at, :] = product[:, n * 128 : (n + 1) * 128]
            away_ref[n, at, :] = product[:, (n + 4) * 128 : (n + 5) * 128]

    steps(near_ref.shape[1], body)


def back_kernel(rows_ref, mine_ref, far_ref, *refs):
    masks, (near_ref, z_ref, half0_ref, half1_ref, kept_ref) = refs[:6], refs[-5:]
    for low, high, _, to in CHUNKS:
        at = slice(low, high)
        weight = jnp.concatenate([ref[n, at, :] for ref in (mine_ref, far_ref) for n in range(4)], axis=1)
        back = matmul_t(rows_ref[...], weight).astype(BF16)
        near_ref[:, at] = back[:128]
        first = jnp.concatenate([ref[:, at] for ref in masks[::2]], axis=0)
        second = jnp.concatenate([ref[:, at] for ref in masks[1::2]], axis=0)
        put_kept(kept_ref, to, back[128:] * first, back[128:] * second, high - low)
    middle = half0_ref.shape[1]
    z_ref[...] = kept_ref[128:256]
    for n in range(2):
        half0_ref[n] = kept_ref[256 * n : 256 * n + middle]
        half1_ref[n] = kept_ref[256 * n + middle : 256 * n + 128]


def added(*arrays):
    total = arrays[0].astype(F32)
    for array in arrays[1:]:
        total = total + array.astype(F32)
    return total


def core_kernel(near_ref, far_ref, *refs):
    send0_ref, send1_ref, sum_ref = refs[-3:]
    middle = send0_ref.shape[1]
    for n in range(2):
        send = added(near_ref[2 * n + 1], far_ref[2 * n + 1]).astype(BF16)
        send0_ref[n] = send[:middle]
        send1_ref[n] = send[middle:]
        sum_ref[n] = added(near_ref[2 * n], far_ref[2 * n])


def x_kernel(first0, first3, first_far, second0, second1, second_far, *refs):
    first_sum, first_send, second_sum, second_send = refs
    first_sum[...] = added(first0[...], first_far[0])
    first_send[...] = added(first3[...], first_far[1]).astype(BF16)
    second_sum[...] = added(second0[...], second_far[0])
    second_send[...] = added(second1[...], second_far[1]).astype(BF16)


def z0_kernel(sum_ref, far0_ref, back_ref, back0_ref, first_ref, first_far, second_ref, second_far, *refs):
    weight1_ref, back1_ref = refs[:2]
    weight_out, back_out, weight1_out, back1_out, first_out, second_out = refs[2:]
    weight_out[...] = added(sum_ref[1, : far0_ref.shape[1]], far0_ref[1]).astype(BF16)
    back_out[...] = added(back_ref[: back0_ref.shape[1]], back0_ref[1]).astype(BF16)
    weight1_out[...] = weight1_ref[...]
    back1_out[...] = back1_ref[...]
    first_out[...] = added(first_ref[...], first_far[...])
    second_out[...] = added(second_ref[...], second_far[...]).astype(BF16)


def z1_kernel(sum_ref, far1_ref, back_ref, back1_ref, first_ref, second_ref, *refs):
    weight_out, back_out, part_refs = refs[-6], refs[-5], refs[-4:]
    middle = sum_ref.shape[1] - far1_ref.shape[1]
    weight_out[...] = added(sum_ref[1, middle:], far1_ref[1]).astype(BF16)
    middle = back_ref.shape[0] - back1_ref.shape[1]
    back_out[...] = added(back_ref[middle:], back1_ref[1]).astype(BF16)
    for n, ref in enumerate(part_refs):
        ref[...] = added(first_ref[n], second_ref[n]).astype(BF16)


def last_kernel(place_ref, *refs):
    sum_ref, far0, far1, z0, z1, back_ref, back0, back1, backz0, backz1 = refs[:10]
    slope_ref, first_ref = refs[10:12]
    parts, (weight_out, input_out, output_ref) = refs[12:16], refs[16:]
    middle = far0.shape[1]
    for at, far, last in ((slice(0, middle), far0, z0), (slice(middle, None), far1, z1)):
        weight_out[at] = added(sum_ref[0, at], far[0], last[...]).astype(BF16)
    middle = back0.shape[1]
    for at, far, last in ((slice(0, middle), back0.at[0], backz0), (slice(middle, None), back1.at[0], backz1)):
        for low, high, _, to in CHUNKS:
            far_0, far_1 = spread_kept(far, to, high - low)
            last_0, last_1 = spread_kept(last, to, high - low)
            arrived = jnp.where(first_ref[at, low:high].astype(F32) > 0.5, far_0 + last_0, far_1 + last_1)
            back = back_ref[at, low:high].astype(F32) + arrived
            input_out[at, low:high] = (slope_ref[at, low:high].astype(F32) * back).astype(BF16)
    me = place_ref[0]
    for part_ref, token in zip(parts, TOKEN_PARTS):
        for n, column in enumerate(COLUMN_BLOCKS):
            at = pl.multiple_of((me ^ (token ^ column)) * 128, 128)
            output_ref[:, pl.ds(at, 128)] = part_ref[:, n * 128 : (n + 1) * 128]


def move(kernel, out_shape, *arrays, scratch=(), flops=COST):
    return call(
        kernel,
        out_shape,
        in_specs=[in_smem() if a.dtype == jnp.int32 and a.size == 1 else whole() for a in arrays],
        out_specs=[whole()] * len(out_shape),
        scratch=scratch,
        flops=flops,
        moved=COST,
    )(*arrays)


def on_device(preactivation, keep_codes, down_weight, output_grad):
    rows, width = preactivation.shape
    scale = 1.0 / math.sqrt(rows * lax.axis_size("dp"))
    dp_place, mp_place = place("dp"), place("mp")

    def shape(*sizes):
        return jax.ShapeDtypeStruct(sizes, BF16)

    def wide(*sizes):
        return jax.ShapeDtypeStruct(sizes, F32)

    piece, column = shape(rows, width), shape(width, 128)
    packed_shape = shape(rows, PACKED)
    half0_shape, half1_shape = shape(FIRST, PACKED), shape(rows - FIRST, PACKED)
    part, pair = shape(4, 16, 1024), shape(2, 4, 16, 1024)
    early = width * EARLY // rows
    split0, split1 = shape(2, early, 128), shape(2, width - early, 128)
    rows_scratch = [pltpu.VMEM((512, 1024), BF16)]

    grad_far = mp_swap(output_grad, 1)
    hidden, slope, first_kept, packed = move(
        mask_kernel,
        [piece, piece, piece, packed_shape],
        preactivation,
        keep_codes.T,
        flops=10**11,
    )
    outs = move(
        first_kernel,
        [shape(2, 16, 1024)] * 4 + [half0_shape, column],
        dp_place,
        output_grad,
        grad_far,
        packed,
        down_weight,
    )
    parts, half_out, weight_out = outs[:4], outs[4], outs[5]

    parts = [parts[0]] + [dp_swap(p, k) for p, k in zip(parts[1:], TOKEN_PARTS[1:])]
    weight_z = dp_swap(weight_out, COLS_Z)
    weight_y = dp_swap(weight_out, COLS_Y)
    hidden_z0 = dp_swap(half_out, ROWS_Z)
    near, far, half_out, hidden_out, weight_out = move(
        second_kernel, [part, part, half1_shape, packed_shape, column], *parts, packed, weight_z, hidden_z0, weight_y
    )

    near_x = mp_swap(near, 2)
    far_x = mp_swap(far, 6)
    hidden_z1 = dp_swap(half_out, ROWS_Z)
    hidden_y = dp_swap(hidden_out, ROWS_Y)
    weight_yz = dp_swap(weight_out, COLS_Y)
    near_two, far_two, hidden_z, weights = move(
        third_kernel,
        [pair, pair, packed_shape, shape(4, width, 128)],
        near,
        near_x,
        far,
        far_x,
        hidden_z0,
        hidden_z1,
        down_weight,
        weight_y,
        weight_z,
        weight_yz,
        hidden_y,
    )

    near_rest = mp_swap(near_two, 6)
    far_rest = mp_swap(far_two, 2)
    hidden_yz = dp_swap(hidden_z, ROWS_Y)
    weights_far = dp_swap(weights, CORE)
    grads = [near_two, near_rest, far_two, far_rest]
    masked = [piece] * 3
    hidden_y, first_y, second_y, hidden_z, first_z, second_z = move(
        unpack_kernel, masked * 2, hidden_y, hidden_z, flops=3 * 10**9
    )
    hidden_yz, first_yz, second_yz = move(unpack_kernel, masked, hidden_yz)
    masks = [first_y, second_y, first_z, second_z, first_yz, second_yz]
    hiddens = [hidden, hidden_y, hidden_z, hidden_yz]

    near, away, grad_rows = move(
        lambda *refs: weight_grad_kernel(scale, *refs),
        [shape(4, width, 128)] * 2 + [shape(512, 1024)],
        mp_place,
        *grads,
        *hiddens,
        flops=5 * 10**9,
    )
    away = dp_swap(away, CORE)
    first0, first3, first_send, second0, second1, second_send = move(
        output_kernel,
        [part, part, pair, part, part, pair],
        mp_place,
        *hiddens,
        weights,
        weights_far,
        near,
        scratch=rows_scratch,
        flops=5 * 10**9,
    )
    first_far = mp_swap(first_send, 2)
    second_far = mp_swap(second_send, 6)
    send0, send1, sums = move(
        core_kernel, [split0, split1, wide(2, width, 128)], near, away, first0
    )
    far0 = dp_swap(send0, COLS_Y)
    back_near, back_z, half0, half1 = move(
        back_kernel,
        [piece, shape(rows, KEPT), shape(2, EARLY, KEPT), shape(2, rows - EARLY, KEPT)],
        grad_rows,
        weights,
        weights_far,
        *masks,
        send0,
        scratch=[pltpu.VMEM((3 * rows, KEPT), BF16)],
        flops=5 * 10**9,
    )
    back0 = dp_swap(half0, ROWS_Y)
    first, first_send, second, second_send = move(
        x_kernel,
        [wide(4, 16, 1024), part] * 2,
        first0,
        first3,
        first_far,
        second0,
        second1,
        second_far,
    )
    first_far = mp_swap(first_send, 6)
    second_far = mp_swap(second_send, 2)

    weight_z0, back_z0, send1, half1, first, second = move(
        z0_kernel,
        [
            shape(early, 128),
            shape(EARLY, KEPT),
            split1,
            shape(2, rows - EARLY, KEPT),
            wide(4, 16, 1024),
            part,
        ],
        sums,
        far0,
        back_z,
        back0,
        first,
        first_far,
        second,
        second_far,
        send1,
        half1,
    )
    weight_z0 = dp_swap(weight_z0, COLS_Z)
    back_z0 = dp_swap(back_z0, ROWS_Z)
    far1 = dp_swap(send1, COLS_Y)
    back1 = dp_swap(half1, ROWS_Y)
    second = mp_swap(second, 1)

    outs = move(
        z1_kernel,
        [shape(width - early, 128), shape(rows - EARLY, KEPT)] + [shape(16, 1024)] * 4,
        sums,
        far1,
        back_z,
        back1,
        first,
        second,
        weight_z0,
        back_z0,
    )
    weight_z1 = dp_swap(outs[0], COLS_Z)
    back_z1 = dp_swap(outs[1], ROWS_Z)
    parts = [outs[2]] + [dp_swap(p, k) for p, k in zip(outs[3:], TOKEN_PARTS[1:])]
    weight_grad, input_grad, output = move(
        last_kernel,
        [column, piece, shape(16, 4096)],
        dp_place,
        sums,
        far0,
        far1,
        weight_z0,
        weight_z1,
        back_near,
        back0,
        back1,
        back_z0,
        back_z1,
        slope,
        first_kept,
        *parts,
    )
    return (output, weight_grad, input_grad)


def solution(mesh):
    in_specs = (P("dp", "mp"), P("dp", "mp"), P("mp", "dp"), P(("dp", "mp"), None))
    out_specs = (P(("dp", "mp"), None), P("mp", "dp"), P("dp", "mp"))
    return jax.shard_map(
        on_device, mesh=mesh, in_specs=in_specs, out_specs=out_specs, check_vma=False
    )
```

```python
import math

import jax
import jax.numpy as jnp
from jax import lax
from jax.experimental import pallas as pl
from jax.experimental.pallas import tpu as pltpu
from jax.sharding import PartitionSpec as P

BF16 = jnp.bfloat16
F32 = jnp.float32

CORE = 1
ROWS_Y, ROWS_Z = 2, 16
COLS_Y, COLS_Z = 6, 8
TOKEN_PARTS = (0, ROWS_Y, ROWS_Z, ROWS_Y ^ ROWS_Z)
COLUMN_PARTS = (0, COLS_Y, COLS_Z, COLS_Y ^ COLS_Z)
COLUMN_BLOCKS = COLUMN_PARTS + tuple(k ^ CORE for k in COLUMN_PARTS)
STEP = 256
COST = 1
PACKED = 3 * 384 + 256
KEPT = 3 * 256 + 128
CHUNKS = ((0, 512, 0, 0), (512, 1024, 384, 256), (1024, 1536, 768, 512), (1536, 1792, 1152, 768))
EARLY = 64
FIRST = 48


def swap(array, axis, size, k):
    return lax.ppermute(array, axis, [(i, i ^ k) for i in range(size)])


def dp_swap(array, k):
    return swap(array, "dp", 32, k)


def mp_swap(array, k):
    return swap(array, "mp", 8, k)


def place(axis):
    return jnp.reshape(lax.axis_index(axis).astype(jnp.int32), (1,))


def in_smem():
    return pl.BlockSpec(memory_space=pltpu.SMEM)


def whole():
    return pl.BlockSpec(memory_space=pltpu.VMEM)


def call(kernel, out_shape, scratch=(), grid=None, in_specs=None, out_specs=None, flops=0, moved=0, limit=12 * 2**20):
    return pl.pallas_call(
        kernel,
        out_shape=out_shape,
        grid=grid or (),
        in_specs=in_specs,
        out_specs=out_specs,
        scratch_shapes=list(scratch),
        compiler_params=pltpu.CompilerParams(vmem_limit_bytes=limit),
        cost_estimate=pl.CostEstimate(flops=flops, bytes_accessed=moved, transcendentals=0),
    )


def spread(rows, width, start=0):
    of = lax.broadcasted_iota(jnp.int32, (rows, width), 1) // 4 + start
    return (of == lax.broadcasted_iota(jnp.int32, (rows, width), 0)).astype(BF16)


def spreads(width):
    if width == 512:
        return spread(128, 512), spread(128, 512)
    return spread(128, 256), spread(128, 256, 64)


def matmul(a, b):
    return jnp.dot(a, b, preferred_element_type=F32)


def matmul_t(a, b):
    return lax.dot_general(a, b, (((1,), (1,)), ((), ())), preferred_element_type=F32)


def kept_places(code):
    first = (code > 2.5).astype(F32) + (code > 4.5).astype(F32)
    second = 3.0 - ((code == 1.0) | (code == 3.0)).astype(F32) - 2.0 * (code == 0.0).astype(F32)
    return first.astype(BF16), second.astype(BF16)


def lanes(shape):
    return (lax.broadcasted_iota(jnp.int32, shape, 1) % 4).astype(F32)


def put_kept(ref, at, kept0, kept1, width):
    to0, to1 = spreads(width)
    if width == 512:
        ref[:, at : at + 128] = matmul_t(kept0, to0).astype(BF16)
        ref[:, at + 128 : at + 256] = matmul_t(kept1, to1).astype(BF16)
    else:
        ref[:, at : at + 128] = (matmul_t(kept0, to0) + matmul_t(kept1, to1)).astype(BF16)


def mask_kernel(pre_ref, code_ref, hidden_ref, slope_ref, first_ref, packed_ref):
    for low, high, at, _ in CHUNKS:
        width = high - low
        code = code_ref[low // 4 : high // 4, :].astype(F32)
        first, second = kept_places(code)
        turn = (((0,), (0,)), ((), ()))
        to = spread(width // 4, width)
        first = lax.dot_general(first, to, turn, preferred_element_type=F32)
        second = lax.dot_general(second, to, turn, preferred_element_type=F32)
        lane = lanes(first.shape)
        is_first, is_second = first == lane, second == lane
        positive = jnp.maximum(pre_ref[:, low:high].astype(F32), 0.0)
        square = positive * positive
        kept0 = jnp.where(is_first, square, 0.0)
        kept1 = jnp.where(is_second, square, 0.0)
        hidden_ref[:, low:high] = (kept0 + kept1).astype(BF16)
        slope_ref[:, low:high] = jnp.where(is_first | is_second, 2.0 * positive, 0.0).astype(BF16)
        first_ref[:, low:high] = jnp.where(is_first, 1.0, 0.0).astype(BF16)
        put_kept(packed_ref, at, kept0.astype(BF16), kept1.astype(BF16), width)
        same = lax.broadcasted_iota(jnp.int32, (width // 4, 128), 0)
        same = (same == lax.broadcasted_iota(jnp.int32, same.shape, 1)).astype(BF16)
        codes = lax.dot_general(code.astype(BF16), same, turn, preferred_element_type=F32)
        at = at + (256 if width == 512 else 128)
        packed_ref[:, at : at + 128] = codes.astype(BF16)


def spread_kept(ref, at, width):
    to0, to1 = spreads(width)
    values = ref[:, at : at + 128]
    others = ref[:, at + 128 : at + 256] if width == 512 else values
    return matmul(values, to0), matmul(others, to1)


def unpack_kernel(*refs):
    count = len(refs) // 4
    for n in range(count):
        packed_ref = refs[n]
        hidden_ref, first_ref, second_ref = refs[count + 3 * n : count + 3 * n + 3]
        for low, high, at, _ in CHUNKS:
            width = high - low
            value0, value1 = spread_kept(packed_ref, at, width)
            at = at + (256 if width == 512 else 128)
            first, second = kept_places(packed_ref[:, at : at + 128].astype(F32))
            to = spreads(width)[0]
            first, second = matmul(first, to), matmul(second, to)
            lane = lanes(first.shape)
            is_first, is_second = first == lane, second == lane
            hidden = jnp.where(is_first, value0, jnp.where(is_second, value1, 0.0))
            hidden_ref[:, low:high] = hidden.astype(BF16)
            first_ref[:, low:high] = jnp.where(is_first, 1.0, 0.0).astype(BF16)
            second_ref[:, low:high] = jnp.where(is_second, 1.0, 0.0).astype(BF16)


def first_kernel(place_ref, grad_ref, grad_far, hidden_ref, weight_ref, *refs):
    part_refs, half_ref, weight_out = refs[-6:-2], refs[-2], refs[-1]
    me = place_ref[0]
    for out_ref, token in zip(part_refs, TOKEN_PARTS):
        for n, column in enumerate(COLUMN_BLOCKS):
            at = pl.ds(pl.multiple_of((me ^ (token ^ column)) * 128, 128), 128)
            out_ref[0, :, n * 128 : (n + 1) * 128] = grad_ref[:, at]
            out_ref[1, :, n * 128 : (n + 1) * 128] = grad_far[:, at]
    half_ref[...] = hidden_ref[: half_ref.shape[0]]
    weight_out[...] = weight_ref[...]


def second_kernel(*refs):
    part_refs, hidden_ref, weight_z = refs[:4], refs[4], refs[5]
    near_ref, far_ref, half_ref, hidden_out, weight_out = refs[-5:]
    for n, ref in enumerate(part_refs):
        near_ref[n] = ref[0]
        far_ref[n] = ref[1]
    half_ref[...] = hidden_ref[hidden_ref.shape[0] - half_ref.shape[0] :]
    hidden_out[...] = hidden_ref[...]
    weight_out[...] = weight_z[...]


def third_kernel(near_ref, near_x, far_ref, far_x, z0_ref, z1_ref, *refs):
    weight_refs = refs[:4]
    near_out, far_out, hidden_z, weights, weights_send = refs[-5:]
    near_out[0] = near_ref[...]
    near_out[1] = near_x[...]
    far_out[0] = far_ref[...]
    far_out[1] = far_x[...]
    hidden_z[: z0_ref.shape[0]] = z0_ref[...]
    hidden_z[z0_ref.shape[0] :] = z1_ref[...]
    for n, ref in enumerate(weight_refs):
        weights[n] = ref[...]
        weights_send[n] = ref[...]


def gather_rows(me, grad_refs, rows_ref):
    near_two, near_rest, far_two, far_rest = grad_refs
    for k in range(4):
        for rx, ref in enumerate((near_two.at[0], near_two.at[1], near_rest.at[1], near_rest.at[0])):
            rows_ref[part_at(me, rx, 0, k), :] = ref[k]
        for rx, ref in enumerate((far_two.at[0], far_rest.at[0], far_rest.at[1], far_two.at[1])):
            rows_ref[part_at(me, rx, 1, k), :] = ref[k]


def part_at(me, rx, rz, k):
    return pl.ds(pl.multiple_of(k * 128 + (me ^ (2 * rx + rz)) * 16, 16), 16)


def steps(width, body):
    for at in range(0, width, STEP):
        body(slice(at, at + STEP))


def output_kernel(place_ref, *refs):
    hidden_refs, (mine_ref, far_ref) = refs[:4], refs[4:6]
    first0, first3, first_send, second0, second1, second_send, rows_ref = refs[-7:]
    hidden = jnp.concatenate([ref[...] for ref in hidden_refs], axis=0)
    for n in range(4):
        ref = (mine_ref, far_ref)[n // 2]
        weight = jnp.concatenate([ref[2 * n % 4], ref[2 * n % 4 + 1]], axis=1)
        total = jnp.dot(hidden, weight, preferred_element_type=F32).astype(BF16)
        rows_ref[:, 256 * n : 256 * (n + 1)] = total
    me = place_ref[0]
    for k in range(4):
        for rx, ref in enumerate((first0, first_send.at[0], first_send.at[1], first3)):
            ref[k] = rows_ref[part_at(me, rx, 0, k), :]
        for rx, ref in enumerate((second0, second1, second_send.at[1], second_send.at[0])):
            ref[k] = rows_ref[part_at(me, rx, 1, k), :]


def weight_grad_kernel(scale, place_ref, *refs):
    grad_refs, hidden_refs, (near_ref, away_ref, rows_ref) = refs[:4], refs[4:8], refs[-3:]
    gather_rows(place_ref[0], grad_refs, rows_ref)

    def body(at):
        hidden = jnp.concatenate([ref[:, at] for ref in hidden_refs], axis=0)
        product = lax.dot_general(
            hidden, rows_ref[...], (((0,), (0,)), ((), ())), preferred_element_type=F32
        )
        product = (product * scale).astype(BF16)
        for n in range(4):
            near_ref[n, at, :] = product[:, n * 128 : (n + 1) * 128]
            away_ref[n, at, :] = product[:, (n + 4) * 128 : (n + 5) * 128]

    steps(near_ref.shape[1], body)


def back_kernel(rows_ref, mine_ref, far_ref, *refs):
    masks, (near_ref, z_ref, half0_ref, half1_ref, kept_ref) = refs[:6], refs[-5:]
    for low, high, _, to in CHUNKS:
        at = slice(low, high)
        weight = jnp.concatenate([ref[n, at, :] for ref in (mine_ref, far_ref) for n in range(4)], axis=1)
        back = matmul_t(rows_ref[...], weight).astype(BF16)
        near_ref[:, at] = back[:128]
        first = jnp.concatenate([ref[:, at] for ref in masks[::2]], axis=0)
        second = jnp.concatenate([ref[:, at] for ref in masks[1::2]], axis=0)
        put_kept(kept_ref, to, back[128:] * first, back[128:] * second, high - low)
    middle = half0_ref.shape[1]
    z_ref[...] = kept_ref[128:256]
    for n in range(2):
        half0_ref[n] = kept_ref[256 * n : 256 * n + middle]
        half1_ref[n] = kept_ref[256 * n + middle : 256 * n + 128]


def added(*arrays):
    total = arrays[0].astype(F32)
    for array in arrays[1:]:
        total = total + array.astype(F32)
    return total


def core_kernel(near_ref, far_ref, *refs):
    send0_ref, send1_ref, sum_ref = refs[-3:]
    middle = send0_ref.shape[1]
    for n in range(2):
        send = added(near_ref[2 * n + 1], far_ref[2 * n + 1]).astype(BF16)
        send0_ref[n] = send[:middle]
        send1_ref[n] = send[middle:]
        sum_ref[n] = added(near_ref[2 * n], far_ref[2 * n])


def x_kernel(first0, first3, first_far, second0, second1, second_far, *refs):
    first_sum, first_send, second_sum, second_send = refs
    first_sum[...] = added(first0[...], first_far[0])
    first_send[...] = added(first3[...], first_far[1]).astype(BF16)
    second_sum[...] = added(second0[...], second_far[0])
    second_send[...] = added(second1[...], second_far[1]).astype(BF16)


def z0_kernel(sum_ref, far0_ref, back_ref, back0_ref, first_ref, first_far, second_ref, second_far, *refs):
    weight1_ref, back1_ref = refs[:2]
    weight_out, back_out, weight1_out, back1_out, first_out, second_out = refs[2:]
    weight_out[...] = added(sum_ref[1, : far0_ref.shape[1]], far0_ref[1]).astype(BF16)
    back_out[...] = added(back_ref[: back0_ref.shape[1]], back0_ref[1]).astype(BF16)
    weight1_out[...] = weight1_ref[...]
    back1_out[...] = back1_ref[...]
    first_out[...] = added(first_ref[...], first_far[...])
    second_out[...] = added(second_ref[...], second_far[...]).astype(BF16)


def z1_kernel(sum_ref, far1_ref, back_ref, back1_ref, first_ref, second_ref, *refs):
    weight_out, back_out, part_refs = refs[-6], refs[-5], refs[-4:]
    middle = sum_ref.shape[1] - far1_ref.shape[1]
    weight_out[...] = added(sum_ref[1, middle:], far1_ref[1]).astype(BF16)
    middle = back_ref.shape[0] - back1_ref.shape[1]
    back_out[...] = added(back_ref[middle:], back1_ref[1]).astype(BF16)
    for n, ref in enumerate(part_refs):
        ref[...] = added(first_ref[n], second_ref[n]).astype(BF16)


def last_kernel(place_ref, *refs):
    sum_ref, far0, far1, z0, z1, back_ref, back0, back1, backz0, backz1 = refs[:10]
    slope_ref, first_ref = refs[10:12]
    parts, (weight_out, input_out, output_ref) = refs[12:16], refs[16:]
    middle = far0.shape[1]
    for at, far, last in ((slice(0, middle), far0, z0), (slice(middle, None), far1, z1)):
        weight_out[at] = added(sum_ref[0, at], far[0], last[...]).astype(BF16)
    middle = back0.shape[1]
    for at, far, last in ((slice(0, middle), back0.at[0], backz0), (slice(middle, None), back1.at[0], backz1)):
        for low, high, _, to in CHUNKS:
            far_0, far_1 = spread_kept(far, to, high - low)
            last_0, last_1 = spread_kept(last, to, high - low)
            arrived = jnp.where(first_ref[at, low:high].astype(F32) > 0.5, far_0 + last_0, far_1 + last_1)
            back = back_ref[at, low:high].astype(F32) + arrived
            input_out[at, low:high] = (slope_ref[at, low:high].astype(F32) * back).astype(BF16)
    me = place_ref[0]
    for part_ref, token in zip(parts, TOKEN_PARTS):
        for n, column in enumerate(COLUMN_BLOCKS):
            at = pl.multiple_of((me ^ (token ^ column)) * 128, 128)
            output_ref[:, pl.ds(at, 128)] = part_ref[:, n * 128 : (n + 1) * 128]


def move(kernel, out_shape, *arrays, scratch=(), flops=COST):
    return call(
        kernel,
        out_shape,
        in_specs=[in_smem() if a.dtype == jnp.int32 and a.size == 1 else whole() for a in arrays],
        out_specs=[whole()] * len(out_shape),
        scratch=scratch,
        flops=flops,
        moved=COST,
    )(*arrays)


def on_device(preactivation, keep_codes, down_weight, output_grad):
    rows, width = preactivation.shape
    scale = 1.0 / math.sqrt(rows * lax.axis_size("dp"))
    dp_place, mp_place = place("dp"), place("mp")

    def shape(*sizes):
        return jax.ShapeDtypeStruct(sizes, BF16)

    def wide(*sizes):
        return jax.ShapeDtypeStruct(sizes, F32)

    piece, column = shape(rows, width), shape(width, 128)
    packed_shape = shape(rows, PACKED)
    half0_shape, half1_shape = shape(FIRST, PACKED), shape(rows - FIRST, PACKED)
    part, pair = shape(4, 16, 1024), shape(2, 4, 16, 1024)
    early = width * EARLY // rows
    split0, split1 = shape(2, early, 128), shape(2, width - early, 128)
    rows_scratch = [pltpu.VMEM((512, 1024), BF16)]

    grad_far = mp_swap(output_grad, 1)
    hidden, slope, first_kept, packed = move(
        mask_kernel,
        [piece, piece, piece, packed_shape],
        preactivation,
        keep_codes.T,
        flops=10**11,
    )
    outs = move(
        first_kernel,
        [shape(2, 16, 1024)] * 4 + [half0_shape, column],
        dp_place,
        output_grad,
        grad_far,
        packed,
        down_weight,
    )
    parts, half_out, weight_out = outs[:4], outs[4], outs[5]

    parts = [parts[0]] + [dp_swap(p, k) for p, k in zip(parts[1:], TOKEN_PARTS[1:])]
    weight_z = dp_swap(weight_out, COLS_Z)
    weight_y = dp_swap(weight_out, COLS_Y)
    hidden_z0 = dp_swap(half_out, ROWS_Z)
    near, far, half_out, hidden_out, weight_out = move(
        second_kernel, [part, part, half1_shape, packed_shape, column], *parts, packed, weight_z, hidden_z0, weight_y
    )

    near_x = mp_swap(near, 2)
    far_x = mp_swap(far, 6)
    hidden_z1 = dp_swap(half_out, ROWS_Z)
    hidden_y = dp_swap(hidden_out, ROWS_Y)
    weight_yz = dp_swap(weight_out, COLS_Y)
    near_two, far_two, hidden_z, weights, weights_send = move(
        third_kernel,
        [pair, pair, packed_shape] + [shape(4, width, 128)] * 2,
        near,
        near_x,
        far,
        far_x,
        hidden_z0,
        hidden_z1,
        down_weight,
        weight_y,
        weight_z,
        weight_yz,
        hidden_y,
    )

    near_rest = mp_swap(near_two, 6)
    far_rest = mp_swap(far_two, 2)
    hidden_yz = dp_swap(hidden_z, ROWS_Y)
    weights_far = dp_swap(weights_send, CORE)
    grads = [near_two, near_rest, far_two, far_rest]
    masked = [piece] * 3
    hidden_y, first_y, second_y, hidden_z, first_z, second_z = move(
        unpack_kernel, masked * 2, hidden_y, hidden_z, flops=3 * 10**9
    )
    hidden_yz, first_yz, second_yz = move(unpack_kernel, masked, hidden_yz)
    masks = [first_y, second_y, first_z, second_z, first_yz, second_yz]
    hiddens = [hidden, hidden_y, hidden_z, hidden_yz]

    near, away, grad_rows = move(
        lambda *refs: weight_grad_kernel(scale, *refs),
        [shape(4, width, 128)] * 2 + [shape(512, 1024)],
        mp_place,
        *grads,
        *hiddens,
        flops=5 * 10**9,
    )
    away = dp_swap(away, CORE)
    first0, first3, first_send, second0, second1, second_send = move(
        output_kernel,
        [part, part, pair, part, part, pair],
        mp_place,
        *hiddens,
        weights,
        weights_far,
        near,
        scratch=rows_scratch,
        flops=5 * 10**9,
    )
    first_far = mp_swap(first_send, 2)
    second_far = mp_swap(second_send, 6)
    send0, send1, sums = move(
        core_kernel, [split0, split1, wide(2, width, 128)], near, away, first0
    )
    far0 = dp_swap(send0, COLS_Y)
    back_near, back_z, half0, half1 = move(
        back_kernel,
        [piece, shape(rows, KEPT), shape(2, EARLY, KEPT), shape(2, rows - EARLY, KEPT)],
        grad_rows,
        weights,
        weights_far,
        *masks,
        send0,
        scratch=[pltpu.VMEM((3 * rows, KEPT), BF16)],
        flops=5 * 10**9,
    )
    back0 = dp_swap(half0, ROWS_Y)
    first, first_send, second, second_send = move(
        x_kernel,
        [wide(4, 16, 1024), part] * 2,
        first0,
        first3,
        first_far,
        second0,
        second1,
        second_far,
    )
    first_far = mp_swap(first_send, 6)
    second_far = mp_swap(second_send, 2)

    weight_z0, back_z0, send1, half1, first, second = move(
        z0_kernel,
        [
            shape(early, 128),
            shape(EARLY, KEPT),
            split1,
            shape(2, rows - EARLY, KEPT),
            wide(4, 16, 1024),
            part,
        ],
        sums,
        far0,
        back_z,
        back0,
        first,
        first_far,
        second,
        second_far,
        send1,
        half1,
    )
    weight_z0 = dp_swap(weight_z0, COLS_Z)
    back_z0 = dp_swap(back_z0, ROWS_Z)
    far1 = dp_swap(send1, COLS_Y)
    back1 = dp_swap(half1, ROWS_Y)
    second = mp_swap(second, 1)

    outs = move(
        z1_kernel,
        [shape(width - early, 128), shape(rows - EARLY, KEPT)] + [shape(16, 1024)] * 4,
        sums,
        far1,
        back_z,
        back1,
        first,
        second,
        weight_z0,
        back_z0,
    )
    weight_z1 = dp_swap(outs[0], COLS_Z)
    back_z1 = dp_swap(outs[1], ROWS_Z)
    parts = [outs[2]] + [dp_swap(p, k) for p, k in zip(outs[3:], TOKEN_PARTS[1:])]
    weight_grad, input_grad, output = move(
        last_kernel,
        [column, piece, shape(16, 4096)],
        dp_place,
        sums,
        far0,
        far1,
        weight_z0,
        weight_z1,
        back_near,
        back0,
        back1,
        back_z0,
        back_z1,
        slope,
        first_kept,
        *parts,
    )
    return (output, weight_grad, input_grad)


def solution(mesh):
    in_specs = (P("dp", "mp"), P("dp", "mp"), P("mp", "dp"), P(("dp", "mp"), None))
    out_specs = (P(("dp", "mp"), None), P("mp", "dp"), P("dp", "mp"))
    return jax.shard_map(
        on_device, mesh=mesh, in_specs=in_specs, out_specs=out_specs, check_vma=False
    )
```

```python
import math

import jax
import jax.numpy as jnp
from jax import lax
from jax.experimental import pallas as pl
from jax.experimental.pallas import tpu as pltpu
from jax.sharding import PartitionSpec as P

BF16 = jnp.bfloat16
F32 = jnp.float32

CORE = 1
ROWS_Y, ROWS_Z = 2, 16
COLS_Y, COLS_Z = 6, 8
TOKEN_PARTS = (0, ROWS_Y, ROWS_Z, ROWS_Y ^ ROWS_Z)
COLUMN_PARTS = (0, COLS_Y, COLS_Z, COLS_Y ^ COLS_Z)
COLUMN_BLOCKS = COLUMN_PARTS + tuple(k ^ CORE for k in COLUMN_PARTS)
STEP = 256
COST = 1
PACKED = 3 * 384 + 256
KEPT = 3 * 256 + 128
CHUNKS = ((0, 512, 0, 0), (512, 1024, 384, 256), (1024, 1536, 768, 512), (1536, 1792, 1152, 768))
EARLY = 64
FIRST = 64


def swap(array, axis, size, k):
    return lax.ppermute(array, axis, [(i, i ^ k) for i in range(size)])


def dp_swap(array, k):
    return swap(array, "dp", 32, k)


def mp_swap(array, k):
    return swap(array, "mp", 8, k)


def place(axis):
    return jnp.reshape(lax.axis_index(axis).astype(jnp.int32), (1,))


def in_smem():
    return pl.BlockSpec(memory_space=pltpu.SMEM)


def whole():
    return pl.BlockSpec(memory_space=pltpu.VMEM)


def call(kernel, out_shape, scratch=(), grid=None, in_specs=None, out_specs=None, flops=0, moved=0, limit=12 * 2**20):
    return pl.pallas_call(
        kernel,
        out_shape=out_shape,
        grid=grid or (),
        in_specs=in_specs,
        out_specs=out_specs,
        scratch_shapes=list(scratch),
        compiler_params=pltpu.CompilerParams(vmem_limit_bytes=limit),
        cost_estimate=pl.CostEstimate(flops=flops, bytes_accessed=moved, transcendentals=0),
    )


def spread(rows, width, start=0):
    of = lax.broadcasted_iota(jnp.int32, (rows, width), 1) // 4 + start
    return (of == lax.broadcasted_iota(jnp.int32, (rows, width), 0)).astype(BF16)


def spreads(width):
    if width == 512:
        return spread(128, 512), spread(128, 512)
    return spread(128, 256), spread(128, 256, 64)


def matmul(a, b):
    return jnp.dot(a, b, preferred_element_type=F32)


def matmul_t(a, b):
    return lax.dot_general(a, b, (((1,), (1,)), ((), ())), preferred_element_type=F32)


def kept_places(code):
    first = (code > 2.5).astype(F32) + (code > 4.5).astype(F32)
    second = 3.0 - ((code == 1.0) | (code == 3.0)).astype(F32) - 2.0 * (code == 0.0).astype(F32)
    return first.astype(BF16), second.astype(BF16)


def lanes(shape):
    return (lax.broadcasted_iota(jnp.int32, shape, 1) % 4).astype(F32)


def put_kept(ref, at, kept0, kept1, width):
    to0, to1 = spreads(width)
    if width == 512:
        ref[:, at : at + 128] = matmul_t(kept0, to0).astype(BF16)
        ref[:, at + 128 : at + 256] = matmul_t(kept1, to1).astype(BF16)
    else:
        ref[:, at : at + 128] = (matmul_t(kept0, to0) + matmul_t(kept1, to1)).astype(BF16)


def mask_kernel(pre_ref, code_ref, hidden_ref, slope_ref, first_ref, packed_ref):
    for low, high, at, _ in CHUNKS:
        width = high - low
        code = code_ref[low // 4 : high // 4, :].astype(F32)
        first, second = kept_places(code)
        turn = (((0,), (0,)), ((), ()))
        to = spread(width // 4, width)
        first = lax.dot_general(first, to, turn, preferred_element_type=F32)
        second = lax.dot_general(second, to, turn, preferred_element_type=F32)
        lane = lanes(first.shape)
        is_first, is_second = first == lane, second == lane
        positive = jnp.maximum(pre_ref[:, low:high].astype(F32), 0.0)
        square = positive * positive
        kept0 = jnp.where(is_first, square, 0.0)
        kept1 = jnp.where(is_second, square, 0.0)
        hidden_ref[:, low:high] = (kept0 + kept1).astype(BF16)
        slope_ref[:, low:high] = jnp.where(is_first | is_second, 2.0 * positive, 0.0).astype(BF16)
        first_ref[:, low:high] = jnp.where(is_first, 1.0, 0.0).astype(BF16)
        put_kept(packed_ref, at, kept0.astype(BF16), kept1.astype(BF16), width)
        same = lax.broadcasted_iota(jnp.int32, (width // 4, 128), 0)
        same = (same == lax.broadcasted_iota(jnp.int32, same.shape, 1)).astype(BF16)
        codes = lax.dot_general(code.astype(BF16), same, turn, preferred_element_type=F32)
        at = at + (256 if width == 512 else 128)
        packed_ref[:, at : at + 128] = codes.astype(BF16)


def spread_kept(ref, at, width):
    to0, to1 = spreads(width)
    values = ref[:, at : at + 128]
    others = ref[:, at + 128 : at + 256] if width == 512 else values
    return matmul(values, to0), matmul(others, to1)


def unpack_kernel(*refs):
    count = len(refs) // 4
    for n in range(count):
        packed_ref = refs[n]
        hidden_ref, first_ref, second_ref = refs[count + 3 * n : count + 3 * n + 3]
        for low, high, at, _ in CHUNKS:
            width = high - low
            value0, value1 = spread_kept(packed_ref, at, width)
            at = at + (256 if width == 512 else 128)
            first, second = kept_places(packed_ref[:, at : at + 128].astype(F32))
            to = spreads(width)[0]
            first, second = matmul(first, to), matmul(second, to)
            lane = lanes(first.shape)
            is_first, is_second = first == lane, second == lane
            hidden = jnp.where(is_first, value0, jnp.where(is_second, value1, 0.0))
            hidden_ref[:, low:high] = hidden.astype(BF16)
            first_ref[:, low:high] = jnp.where(is_first, 1.0, 0.0).astype(BF16)
            second_ref[:, low:high] = jnp.where(is_second, 1.0, 0.0).astype(BF16)


def first_kernel(place_ref, grad_ref, grad_far, hidden_ref, weight_ref, *refs):
    part_refs, half_ref, weight_out = refs[-6:-2], refs[-2], refs[-1]
    me = place_ref[0]
    for out_ref, token in zip(part_refs, TOKEN_PARTS):
        for n, column in enumerate(COLUMN_BLOCKS):
            at = pl.ds(pl.multiple_of((me ^ (token ^ column)) * 128, 128), 128)
            out_ref[0, :, n * 128 : (n + 1) * 128] = grad_ref[:, at]
            out_ref[1, :, n * 128 : (n + 1) * 128] = grad_far[:, at]
    half_ref[...] = hidden_ref[: half_ref.shape[0]]
    weight_out[...] = weight_ref[...]


def second_kernel(*refs):
    part_refs, hidden_ref, weight_z = refs[:4], refs[4], refs[5]
    near_ref, far_ref, half_ref, hidden_out, weight_out = refs[-5:]
    for n, ref in enumerate(part_refs):
        near_ref[n] = ref[0]
        far_ref[n] = ref[1]
    half_ref[...] = hidden_ref[hidden_ref.shape[0] - half_ref.shape[0] :]
    hidden_out[...] = hidden_ref[...]
    weight_out[...] = weight_z[...]


def third_kernel(near_ref, near_x, far_ref, far_x, z0_ref, z1_ref, *refs):
    weight_refs = refs[:4]
    near_out, far_out, hidden_z, weights = refs[-4:]
    near_out[0] = near_ref[...]
    near_out[1] = near_x[...]
    far_out[0] = far_ref[...]
    far_out[1] = far_x[...]
    hidden_z[: z0_ref.shape[0]] = z0_ref[...]
    hidden_z[z0_ref.shape[0] :] = z1_ref[...]
    for n, ref in enumerate(weight_refs):
        weights[n] = ref[...]


def gather_rows(me, grad_refs, rows_ref):
    near_two, near_rest, far_two, far_rest = grad_refs
    for k in range(4):
        for rx, ref in enumerate((near_two.at[0], near_two.at[1], near_rest.at[1], near_rest.at[0])):
            rows_ref[part_at(me, rx, 0, k), :] = ref[k]
        for rx, ref in enumerate((far_two.at[0], far_rest.at[0], far_rest.at[1], far_two.at[1])):
            rows_ref[part_at(me, rx, 1, k), :] = ref[k]


def part_at(me, rx, rz, k):
    return pl.ds(pl.multiple_of(k * 128 + (me ^ (2 * rx + rz)) * 16, 16), 16)


def steps(width, body):
    for at in range(0, width, STEP):
        body(slice(at, at + STEP))


def output_kernel(place_ref, *refs):
    hidden_refs, (mine_ref, far_ref) = refs[:4], refs[4:6]
    first0, first3, first_send, second0, second1, second_send, rows_ref = refs[-7:]
    hidden = jnp.concatenate([ref[...] for ref in hidden_refs], axis=0)
    for n in range(4):
        ref = (mine_ref, far_ref)[n // 2]
        weight = jnp.concatenate([ref[2 * n % 4], ref[2 * n % 4 + 1]], axis=1)
        total = jnp.dot(hidden, weight, preferred_element_type=F32).astype(BF16)
        rows_ref[:, 256 * n : 256 * (n + 1)] = total
    me = place_ref[0]
    for k in range(4):
        for rx, ref in enumerate((first0, first_send.at[0], first_send.at[1], first3)):
            ref[k] = rows_ref[part_at(me, rx, 0, k), :]
        for rx, ref in enumerate((second0, second1, second_send.at[1], second_send.at[0])):
            ref[k] = rows_ref[part_at(me, rx, 1, k), :]


def weight_grad_kernel(scale, place_ref, *refs):
    grad_refs, hidden_refs, (near_ref, away_ref, rows_ref) = refs[:4], refs[4:8], refs[-3:]
    gather_rows(place_ref[0], grad_refs, rows_ref)

    def body(at):
        hidden = jnp.concatenate([ref[:, at] for ref in hidden_refs], axis=0)
        product = lax.dot_general(
            hidden, rows_ref[...], (((0,), (0,)), ((), ())), preferred_element_type=F32
        )
        product = (product * scale).astype(BF16)
        for n in range(4):
            near_ref[n, at, :] = product[:, n * 128 : (n + 1) * 128]
            away_ref[n, at, :] = product[:, (n + 4) * 128 : (n + 5) * 128]

    steps(near_ref.shape[1], body)


def back_kernel(rows_ref, mine_ref, far_ref, *refs):
    masks, (near_ref, z_ref, half0_ref, half1_ref, kept_ref) = refs[:6], refs[-5:]
    for low, high, _, to in CHUNKS:
        at = slice(low, high)
        weight = jnp.concatenate([ref[n, at, :] for ref in (mine_ref, far_ref) for n in range(4)], axis=1)
        back = matmul_t(rows_ref[...], weight).astype(BF16)
        near_ref[:, at] = back[:128]
        first = jnp.concatenate([ref[:, at] for ref in masks[::2]], axis=0)
        second = jnp.concatenate([ref[:, at] for ref in masks[1::2]], axis=0)
        put_kept(kept_ref, to, back[128:] * first, back[128:] * second, high - low)
    middle = half0_ref.shape[1]
    z_ref[...] = kept_ref[128:256]
    for n in range(2):
        half0_ref[n] = kept_ref[256 * n : 256 * n + middle]
        half1_ref[n] = kept_ref[256 * n + middle : 256 * n + 128]


def added(*arrays):
    total = arrays[0].astype(F32)
    for array in arrays[1:]:
        total = total + array.astype(F32)
    return total


def core_kernel(near_ref, far_ref, *refs):
    send0_ref, send1_ref, sum_ref = refs[-3:]
    middle = send0_ref.shape[1]
    for n in range(2):
        send = added(near_ref[2 * n + 1], far_ref[2 * n + 1]).astype(BF16)
        send0_ref[n] = send[:middle]
        send1_ref[n] = send[middle:]
        sum_ref[n] = added(near_ref[2 * n], far_ref[2 * n])


def x_kernel(first0, first3, first_far, second0, second1, second_far, *refs):
    first_sum, first_send, second_sum, second_send = refs
    first_sum[...] = added(first0[...], first_far[0])
    first_send[...] = added(first3[...], first_far[1]).astype(BF16)
    second_sum[...] = added(second0[...], second_far[0])
    second_send[...] = added(second1[...], second_far[1]).astype(BF16)


def z0_kernel(sum_ref, far0_ref, back_ref, back0_ref, first_ref, first_far, second_ref, second_far, *refs):
    weight1_ref, back1_ref = refs[:2]
    weight_out, back_out, weight1_out, back1_out, first_out, second_out = refs[2:]
    weight_out[...] = added(sum_ref[1, : far0_ref.shape[1]], far0_ref[1]).astype(BF16)
    back_out[...] = added(back_ref[: back0_ref.shape[1]], back0_ref[1]).astype(BF16)
    weight1_out[...] = weight1_ref[...]
    back1_out[...] = back1_ref[...]
    first_out[...] = added(first_ref[...], first_far[...])
    second_out[...] = added(second_ref[...], second_far[...]).astype(BF16)


def z1_kernel(sum_ref, far1_ref, back_ref, back1_ref, first_ref, second_ref, *refs):
    weight_out, back_out, part_refs = refs[-6], refs[-5], refs[-4:]
    middle = sum_ref.shape[1] - far1_ref.shape[1]
    weight_out[...] = added(sum_ref[1, middle:], far1_ref[1]).astype(BF16)
    middle = back_ref.shape[0] - back1_ref.shape[1]
    back_out[...] = added(back_ref[middle:], back1_ref[1]).astype(BF16)
    for n, ref in enumerate(part_refs):
        ref[...] = added(first_ref[n], second_ref[n]).astype(BF16)


def last_kernel(place_ref, *refs):
    sum_ref, far0, far1, z0, z1, back_ref, back0, back1, backz0, backz1 = refs[:10]
    slope_ref, first_ref = refs[10:12]
    parts, (weight_out, input_out, output_ref) = refs[12:16], refs[16:]
    middle = far0.shape[1]
    for at, far, last in ((slice(0, middle), far0, z0), (slice(middle, None), far1, z1)):
        weight_out[at] = added(sum_ref[0, at], far[0], last[...]).astype(BF16)
    middle = back0.shape[1]
    for at, far, last in ((slice(0, middle), back0.at[0], backz0), (slice(middle, None), back1.at[0], backz1)):
        for low, high, _, to in CHUNKS:
            far_0, far_1 = spread_kept(far, to, high - low)
            last_0, last_1 = spread_kept(last, to, high - low)
            arrived = jnp.where(first_ref[at, low:high].astype(F32) > 0.5, far_0 + last_0, far_1 + last_1)
            back = back_ref[at, low:high].astype(F32) + arrived
            input_out[at, low:high] = (slope_ref[at, low:high].astype(F32) * back).astype(BF16)
    me = place_ref[0]
    for part_ref, token in zip(parts, TOKEN_PARTS):
        for n, column in enumerate(COLUMN_BLOCKS):
            at = pl.multiple_of((me ^ (token ^ column)) * 128, 128)
            output_ref[:, pl.ds(at, 128)] = part_ref[:, n * 128 : (n + 1) * 128]


def move(kernel, out_shape, *arrays, scratch=(), flops=COST):
    return call(
        kernel,
        out_shape,
        in_specs=[in_smem() if a.dtype == jnp.int32 and a.size == 1 else whole() for a in arrays],
        out_specs=[whole()] * len(out_shape),
        scratch=scratch,
        flops=flops,
        moved=COST,
    )(*arrays)


def on_device(preactivation, keep_codes, down_weight, output_grad):
    rows, width = preactivation.shape
    scale = 1.0 / math.sqrt(rows * lax.axis_size("dp"))
    dp_place, mp_place = place("dp"), place("mp")

    def shape(*sizes):
        return jax.ShapeDtypeStruct(sizes, BF16)

    def wide(*sizes):
        return jax.ShapeDtypeStruct(sizes, F32)

    piece, column = shape(rows, width), shape(width, 128)
    packed_shape = shape(rows, PACKED)
    half0_shape, half1_shape = shape(FIRST, PACKED), shape(rows - FIRST, PACKED)
    part, pair = shape(4, 16, 1024), shape(2, 4, 16, 1024)
    early = width * EARLY // rows
    split0, split1 = shape(2, early, 128), shape(2, width - early, 128)
    rows_scratch = [pltpu.VMEM((512, 1024), BF16)]

    grad_far = mp_swap(output_grad, 1)
    hidden, slope, first_kept, packed = move(
        mask_kernel,
        [piece, piece, piece, packed_shape],
        preactivation,
        keep_codes.T,
        flops=10**11,
    )
    outs = move(
        first_kernel,
        [shape(2, 16, 1024)] * 4 + [half0_shape, column],
        dp_place,
        output_grad,
        grad_far,
        packed,
        down_weight,
    )
    parts, half_out, weight_out = outs[:4], outs[4], outs[5]

    parts = [parts[0]] + [dp_swap(p, k) for p, k in zip(parts[1:], TOKEN_PARTS[1:])]
    weight_z = dp_swap(weight_out, COLS_Z)
    weight_y = dp_swap(weight_out, COLS_Y)
    hidden_z0 = dp_swap(half_out, ROWS_Z)
    near, far, half_out, hidden_out, weight_out = move(
        second_kernel, [part, part, half1_shape, packed_shape, column], *parts, packed, weight_z, hidden_z0, weight_y
    )

    near_x = mp_swap(near, 2)
    far_x = mp_swap(far, 6)
    hidden_z1 = dp_swap(half_out, ROWS_Z)
    hidden_y = dp_swap(hidden_out, ROWS_Y)
    weight_yz = dp_swap(weight_out, COLS_Y)
    near_two, far_two, hidden_z, weights = move(
        third_kernel,
        [pair, pair, packed_shape, shape(4, width, 128)],
        near,
        near_x,
        far,
        far_x,
        hidden_z0,
        hidden_z1,
        down_weight,
        weight_y,
        weight_z,
        weight_yz,
        hidden_y,
    )

    near_rest = mp_swap(near_two, 6)
    far_rest = mp_swap(far_two, 2)
    hidden_yz = dp_swap(hidden_z, ROWS_Y)
    weights_far = dp_swap(weights, CORE)
    grads = [near_two, near_rest, far_two, far_rest]
    masked = [piece] * 3
    hidden_y, first_y, second_y, hidden_z, first_z, second_z = move(
        unpack_kernel, masked * 2, hidden_y, hidden_z, flops=3 * 10**9
    )
    hidden_yz, first_yz, second_yz = move(unpack_kernel, masked, hidden_yz)
    masks = [first_y, second_y, first_z, second_z, first_yz, second_yz]
    hiddens = [hidden, hidden_y, hidden_z, hidden_yz]

    near, away, grad_rows = move(
        lambda *refs: weight_grad_kernel(scale, *refs),
        [shape(4, width, 128)] * 2 + [shape(512, 1024)],
        mp_place,
        *grads,
        *hiddens,
        flops=5 * 10**9,
    )
    away = dp_swap(away, CORE)
    first0, first3, first_send, second0, second1, second_send = move(
        output_kernel,
        [part, part, pair, part, part, pair],
        mp_place,
        *hiddens,
        weights,
        weights_far,
        near,
        scratch=rows_scratch,
        flops=5 * 10**9,
    )
    first_far = mp_swap(first_send, 2)
    second_far = mp_swap(second_send, 6)
    send0, send1, sums = move(
        core_kernel, [split0, split1, wide(2, width, 128)], near, away, first0
    )
    far0 = dp_swap(send0, COLS_Y)
    back_near, back_z, half0, half1 = move(
        back_kernel,
        [piece, shape(rows, KEPT), shape(2, EARLY, KEPT), shape(2, rows - EARLY, KEPT)],
        grad_rows,
        weights,
        weights_far,
        *masks,
        send0,
        scratch=[pltpu.VMEM((3 * rows, KEPT), BF16)],
        flops=5 * 10**9,
    )
    back0 = dp_swap(half0, ROWS_Y)
    first, first_send, second, second_send = move(
        x_kernel,
        [wide(4, 16, 1024), part] * 2,
        first0,
        first3,
        first_far,
        second0,
        second1,
        second_far,
    )
    first_far = mp_swap(first_send, 6)
    second_far = mp_swap(second_send, 2)

    weight_z0, back_z0, send1, half1, first, second = move(
        z0_kernel,
        [
            shape(early, 128),
            shape(EARLY, KEPT),
            split1,
            shape(2, rows - EARLY, KEPT),
            wide(4, 16, 1024),
            part,
        ],
        sums,
        far0,
        back_z,
        back0,
        first,
        first_far,
        second,
        second_far,
        send1,
        half1,
    )
    weight_z0 = dp_swap(weight_z0, COLS_Z)
    back_z0 = dp_swap(back_z0, ROWS_Z)
    far1 = dp_swap(send1, COLS_Y)
    back1 = dp_swap(half1, ROWS_Y)
    second = mp_swap(second, 1)

    outs = move(
        z1_kernel,
        [shape(width - early, 128), shape(rows - EARLY, KEPT)] + [shape(16, 1024)] * 4,
        sums,
        far1,
        back_z,
        back1,
        first,
        second,
        weight_z0,
        back_z0,
    )
    weight_z1 = dp_swap(outs[0], COLS_Z)
    back_z1 = dp_swap(outs[1], ROWS_Z)
    parts = [outs[2]] + [dp_swap(p, k) for p, k in zip(outs[3:], TOKEN_PARTS[1:])]
    weight_grad, input_grad, output = move(
        last_kernel,
        [column, piece, shape(16, 4096)],
        dp_place,
        sums,
        far0,
        far1,
        weight_z0,
        weight_z1,
        back_near,
        back0,
        back1,
        back_z0,
        back_z1,
        slope,
        first_kept,
        *parts,
    )
    return (output, weight_grad, input_grad)


def solution(mesh):
    in_specs = (P("dp", "mp"), P("dp", "mp"), P("mp", "dp"), P(("dp", "mp"), None))
    out_specs = (P(("dp", "mp"), None), P("mp", "dp"), P("dp", "mp"))
    return jax.shard_map(
        on_device, mesh=mesh, in_specs=in_specs, out_specs=out_specs, check_vma=False
    )
```
